512 devices in a mesh: dp: 8 (over z_lo, core), expert: 64 (over z_hi, y, x).
Axes of the slice: x: 4, y: 8, z: 8 (z_hi: 2, z_lo: 4; z = z_hi * 4 + z_lo), core: 2. Of those that a mesh axis runs over, the one named last changes fastest.
Arguments:
- tokens: bfloat16 [2, 2048, 4096], P(None, 'expert', 'dp'), may hold values from -6 to 6
- w_gate: bfloat16 [64, 1536, 4096], P('expert', 'dp'), may hold values from -0.09375 to 0.09375
- w_down: bfloat16 [64, 1536, 4096], P('expert', 'dp'), may hold values from -0.15625 to 0.15625
- expert_ids: int32 [2, 2048, 8], P(None, 'expert'), may hold values from 0 to 63, all different within a row
- route_weight: float32 [2, 2048, 8], P(None, 'expert'), may hold values from 0.1 to 1
- replica_pick: int32 [2, 2048, 8], P(None, 'expert'), may hold values from 0 to 63
- old_plan: int32 [64], replicated, may hold values from 0 to 63, each once
- new_plan: int32 [64], replicated, may hold values from 0 to 63, each once
Outputs:
- layer_out: bfloat16 [2, 2048, 4096], P(None, 'expert', 'dp')
The draws below stay inside these ranges and needn't reach their ends.
Inputs may be any that keep to these rules, and one draw needn't show every extreme that they name: `expert_ids`: each token names 8 different experts, and every expert is named by some token. `old_plan`: each expert stands in exactly one host's second slot. `new_plan`: each expert stands in exactly one host's second slot.
All inputs are finite; a program needn't handle non-finite values.
Results may differ from the reference program's by a relative error of at most 0.02.
Values may be sent and summed in bfloat16 or wider, within the bound.
No kernel may reach another device: no remote copies, remote signals or barrier semaphores. Data moves between devices by JAX's collectives and lax.ppermute only.
A program may use at most 64 MiB of HBM per device.

```python
import math
import jax
import jax.numpy as jnp
from jax import lax

D = 4096
FF = 1536
TOPK = 8
TOK_GRP = 32
EXPERTS = 64
CAP = 4
TOKENS = 2048
N_DP = 8
N_EXPERT = 64


def with_ends(values, own_key, low, high):
    longest = values.shape.index(max(values.shape))
    spots = []
    for shift in (0, 1):
        where = [jax.random.randint(jax.random.fold_in(own_key, axis), (), 0, length) for axis, length in enumerate(values.shape)]
        where[longest] = (where[longest] + shift) % values.shape[longest]
        spots.append(tuple(where))
    return values.at[spots[0]].set(low).at[spots[1]].set(high)


def levels(own_key, dims, split, low, largest):
    loudness = 1.0
    for axis_at, shards_of in split:
        steps = jax.random.uniform(jax.random.fold_in(jax.random.fold_in(own_key, 6), axis_at), (shards_of,), jnp.float32, low / len(split), largest / len(split))
        loudness = loudness * jnp.repeat(jnp.exp(steps), dims[axis_at] // shards_of).reshape((-1,) + (1,) * (len(dims) - 1 - axis_at))
    return loudness


def different_ones(rng, rows, count, top, lift):
    order = jax.random.permutation(jax.random.fold_in(rng, 1), count)
    pull = order
    for power in range(3):
        pull = pull * pull // count
    pull = pull * lift // count
    lots = jax.random.randint(jax.random.fold_in(rng, 2), (rows, count), 0, 4096) + pull
    fixed_rows = jax.random.permutation(jax.random.fold_in(rng, 3), rows)[jnp.arange(count) % rows]
    lots = jnp.where(jnp.arange(rows)[:, None] == fixed_rows[None, :], 1 << 14, lots)
    priority = lots * count + jnp.arange(count)
    return lax.top_k(priority.astype(jnp.int32), top)[1].astype(jnp.int32)


def normal_values(own_key, dims, spread, reach, split=(), held_as=jnp.bfloat16):
    result = jax.random.normal(own_key, dims, jnp.float32) * spread
    if len(split) > 0:
        result = levels(own_key, dims, split, -0.22, 0.18) * result
    return jnp.clip(result, min=-reach, max=reach).astype(held_as)


def setup_inputs(seed: int = 0) -> dict:
    key_list = jax.random.split(jax.random.key(seed), 9)
    return {
        "tokens": normal_values(key_list[0], (2, TOKENS, D), 1.0, 6.0, ((1, 64), (2, 8))),
        "w_gate": normal_values(key_list[1], (EXPERTS, FF, D), D ** -0.5, 0.09375, ((0, 64), (1, 8))),
        "w_down": normal_values(key_list[2], (EXPERTS, FF, D), FF ** -0.5, 0.15625, ((0, 64), (1, 8))),
        "expert_ids": different_ones(key_list[3], 2 * TOKENS, EXPERTS, TOPK, 2048).reshape((2, TOKENS, TOPK)),
        "route_weight": jnp.clip(jnp.exp(math.log(1.0) - 2.3025851 * jax.random.uniform(key_list[4], (2, TOKENS, TOPK), jnp.float32) ** levels(key_list[4], (2, TOKENS, TOPK), ((1, 64),), -0.2, 0.2)), 0.1, 1.0),
        "replica_pick": with_ends(jax.random.randint(key_list[5], (2, TOKENS, TOPK), 0, EXPERTS), jax.random.fold_in(key_list[5], 1), 0, EXPERTS - 1).astype(jnp.int32),
        "old_plan": jax.random.permutation(key_list[6], EXPERTS).astype(jnp.int32),
        "new_plan": jax.random.permutation(key_list[7], EXPERTS).astype(jnp.int32),
    }


def route_rows(placement, expert_ids, replica_pick):
    host_count = placement.shape[0]
    host_ids = jnp.arange(host_count, dtype=jnp.int32)
    same_plan = placement[:, None] == placement[None, :]
    before = host_ids[None, :] < host_ids[:, None]
    copy_rank = 1 + jnp.sum((same_plan & before).astype(jnp.int32), axis=1)
    copies = 1 + jnp.sum((placement[None, :] == host_ids[:, None]).astype(jnp.int32), axis=1)
    flat_ids = expert_ids.reshape(-1)
    flat_pick = replica_pick.reshape(-1)
    named_by = flat_ids[:, None] == host_ids[None, :]
    copy_count = jnp.sum(jnp.where(named_by, copies[None, :], 0), axis=1)
    replica = flat_pick % copy_count
    matched = (placement[None, :] == flat_ids[:, None]) & (copy_rank[None, :] == replica[:, None])
    second = jnp.sum(jnp.where(matched, host_ids[None, :], 0), axis=1)
    target = jnp.where(replica == 0, flat_ids, second)
    spare_slot = (replica > 0).astype(jnp.int32)
    landed = (target[:, None] == host_ids[None, :]).astype(jnp.int32)
    earlier = jnp.cumsum(landed, axis=0) - landed
    position = jnp.sum(earlier * landed, axis=1)
    return target, spare_slot, position


def expert(rows_in, gate_rows, down_rows):
    gate_pre = jnp.dot(rows_in, gate_rows.T, preferred_element_type=jnp.float32)
    hidden = jax.nn.silu(gate_pre).astype(jnp.bfloat16)
    block = FF // N_DP
    total = jnp.zeros((rows_in.shape[0], D), jnp.float32)
    for block_index in range(N_DP):
        partial_term = jnp.dot(hidden[:, block_index * block:(block_index + 1) * block], down_rows[block_index * block:(block_index + 1) * block], preferred_element_type=jnp.float32)
        rounded = lax.optimization_barrier(partial_term.astype(jnp.bfloat16))
        total = total + rounded.astype(jnp.float32)
    return total


def reference(tokens, w_gate, w_down, expert_ids, route_weight, replica_pick, old_plan, new_plan):
    host_count = N_EXPERT
    slot_count = host_count * CAP
    spill_index = host_count * slot_count
    outputs = []
    for batch_index, placement in ((0, old_plan), (1, new_plan)):
        activations = tokens[batch_index].reshape(host_count, TOK_GRP, D)
        chosen = expert_ids[batch_index].reshape(host_count, TOK_GRP, TOPK)
        replica_choice = replica_pick[batch_index].reshape(host_count, TOK_GRP, TOPK)
        target, spare_slot, position = jax.vmap(route_rows, in_axes=(None, 0, 0))(placement, chosen, replica_choice)
        is_kept = position < CAP
        group_ids = jnp.arange(host_count, dtype=jnp.int32)[:, None]
        destination = jnp.where(is_kept, target * slot_count + group_ids * CAP + position, spill_index).reshape(-1)
        source_rows = jnp.repeat(activations, TOPK, axis=1).reshape(-1, D)
        buffers = jnp.zeros((spill_index + 1, D), jnp.bfloat16).at[destination].set(source_rows)
        slot_flags = jnp.zeros((spill_index + 1,), jnp.int32).at[destination].set((spare_slot + 1).reshape(-1))
        buffers = buffers[:spill_index].reshape(host_count, slot_count, D)
        slot_flags = slot_flags[:spill_index].reshape(host_count, slot_count)

        def per_host(inputs):
            host_index, rows_in, flag_row = inputs
            spare_expert = placement[host_index]
            own_out = expert(rows_in, w_gate[host_index], w_down[host_index])
            spare_out = expert(rows_in, w_gate[spare_expert], w_down[spare_expert])
            return jnp.where(flag_row[:, None] == 2, spare_out, own_out).astype(jnp.bfloat16)

        results = lax.map(per_host, (jnp.arange(host_count, dtype=jnp.int32), buffers, slot_flags))
        results = jnp.concatenate([results.reshape(spill_index, D), jnp.zeros((1, D), jnp.bfloat16)], axis=0)
        gathered = results[destination].reshape(host_count, TOK_GRP, TOPK, D).astype(jnp.float32)
        weights = route_weight[batch_index].reshape(host_count, TOK_GRP, TOPK, 1)
        combined = jnp.sum(weights * gathered, axis=2)
        outputs.append(combined.reshape(TOKENS, D).astype(jnp.bfloat16))
    return jnp.stack(outputs)
```

```python
import jax
import jax.numpy as jnp
from jax import lax
from jax.sharding import Mesh
from jax.sharding import PartitionSpec as P

TOPK = 8
CAP = 4
BF = jnp.bfloat16
F32 = jnp.float32

SPLIT = (("p", 2), ("m", 2), ("k", 2), ("zh", 2), ("y", 8), ("x", 4))
MK = ("m", "k")


def dot(a, b, dims, out=F32):
    return lax.dot_general(a, b, (dims, ((), ())), preferred_element_type=out)


def swap(array, dm, dk):
    flip = 2 * dm + dk
    return lax.ppermute(array, MK, [(i, i ^ flip) for i in range(4)])


def recut(weight):
    m, k = lax.axis_index("m"), lax.axis_index("k")
    hidden, feats = weight.shape
    blocks = weight.reshape(hidden, 2, 2, 2, feats // 8)

    def part(dm, dk):
        taken = lax.dynamic_slice(
            blocks, (0, 0, m ^ dm, k ^ dk, 0), (hidden, 2, 1, 1, feats // 8)
        ).reshape(hidden, feats // 4)
        return swap(taken, dm, dk) if dm + dk else taken

    def both(dk):
        same, other = part(0, dk), part(1, dk)
        first = jnp.where(m == 0, same, other)
        second = jnp.where(m == 0, other, same)
        return jnp.concatenate([first, second], axis=0)

    return both(0), both(1)


def slots(codes, weights, plan):
    groups, rows = codes.shape
    hosts = plan.shape[0]
    nx = lax.axis_size("x")
    first = (lax.axis_index("zh") * lax.axis_size("y") + lax.axis_index("y")) * nx
    experts = first + jnp.arange(nx, dtype=jnp.int32)
    ids = jnp.arange(hosts, dtype=jnp.int32)
    spare_host = jnp.sum(jnp.where(plan[None, :] == experts[:, None], ids[None, :], 0), axis=1)
    here = jnp.sum(jnp.where(ids[None, :] == experts[:, None], plan[None, :], 0), axis=1)
    own_code = 2 * jnp.concatenate([experts, spare_host])
    spare_code = 2 * jnp.concatenate([here, experts]) + 1
    is_own = codes[:, None, :] == own_code[None, :, None]
    is_spare = codes[:, None, :] == spare_code[None, :, None]
    landed = is_own | is_spare
    at = jnp.arange(rows, dtype=jnp.int32)
    before = (at[:, None] < at[None, :]).astype(BF)
    position = dot(landed.astype(BF), before, ((2,), (0,)))
    fits = position < CAP
    kept = (is_own[:, :nx] & fits[:, :nx]) | (is_spare[:, nx:] & fits[:, nx:])
    rank = dot(kept.astype(BF), before, ((2,), (0,)))
    slot = jnp.arange(2 * CAP, dtype=F32)
    hit = kept[:, :, None, :] & (rank[:, :, None, :] == slot[None, None, :, None])
    token = at // TOPK + 1
    tokens_of = jnp.sum(jnp.where(hit, token[None, None, None, :], 0), axis=3)
    group = jnp.arange(groups, dtype=jnp.int32)[:, None, None]
    tokens_of = jnp.where(tokens_of > 0, tokens_of - 1 + group * (rows // TOPK), -1)
    weight_of = jnp.sum(jnp.where(hit, weights[:, None, None, :], 0.0), axis=3)
    order = lambda v: v.transpose(1, 0, 2).reshape(-1)
    return order(tokens_of), order(weight_of)


def local(tokens, w_gate, w_down, expert_ids, route_weight, replica_pick, old_plan, new_plan):
    batches, group, feats = tokens.shape
    nx = lax.axis_size("x")
    code = (2 * expert_ids + (replica_pick & 1)).astype(F32)
    info = jnp.stack([code, route_weight]).reshape(2, batches, group * TOPK)
    info = lax.all_gather(info, ("y", "zh"))

    cut = lax.all_gather(tokens, ("zh", "p"))
    cut = cut.reshape(2, 2, batches, group, feats).transpose(2, 0, 3, 1, 4)
    cut = cut.reshape(batches, 2 * group, 2 * feats)

    gate_own, gate_other = recut(w_gate[0])
    down_own, down_other = recut(w_down[0])

    outputs = []
    for index, plan in ((0, old_plan), (1, new_plan)):
        tok = lax.all_gather(cut[index], "y", axis=0, tiled=True)
        codes = info[:, 0, index].astype(jnp.int32)
        slot_token, slot_weight = slots(codes, info[:, 1, index], plan)
        pick = slot_token[:, None] == jnp.arange(tok.shape[0], dtype=jnp.int32)[None, :]
        rows = dot(pick.astype(BF), tok, ((1,), (0,)), BF)
        rows = rows.reshape(nx, -1, rows.shape[1])
        rows = lax.all_to_all(rows, "x", 0, 0, tiled=True).reshape(-1, rows.shape[2])

        send = dot(rows, gate_other, ((1,), (1,)), BF)
        part = dot(rows, gate_own, ((1,), (1,)))
        part = part + swap(send, 0, 1).astype(F32)
        gate = part + swap(part.astype(BF), 1, 0).astype(F32)
        hidden = jax.nn.silu(gate).astype(BF)
        hidden_other = swap(hidden, 0, 1)
        out = dot(hidden, down_own, ((1,), (0,))) + dot(hidden_other, down_other, ((1,), (0,)))
        out = out.astype(BF).reshape(nx, -1, out.shape[1])
        back = lax.all_to_all(out, "x", 0, 0, tiled=True).reshape(-1, out.shape[2])

        scale = jnp.where(pick, slot_weight[:, None], 0.0)
        high = scale.astype(BF)
        low = (scale - high.astype(F32)).astype(BF)
        mixed = dot(high, back, ((0,), (0,))) + dot(low, back, ((0,), (0,)))
        outputs.append(lax.psum_scatter(mixed.astype(BF), "y", scatter_dimension=0, tiled=True))

    mixed = jnp.stack(outputs).reshape(batches, 2, group, 2, feats)
    mixed = mixed.transpose(1, 3, 0, 2, 4).reshape(4, batches, group, feats)
    return lax.psum_scatter(mixed, ("zh", "p"), scatter_dimension=0, tiled=False)


def solution(mesh):
    names = tuple(name for name, _ in SPLIT)
    cut = Mesh(mesh.devices.reshape([size for _, size in SPLIT]), names)
    dp, expert = ("p", "m", "k"), ("zh", "y", "x")
    placed = (
        P(None, expert, dp),
        P(expert, dp, None),
        P(expert, dp, None),
        P(None, expert, None),
        P(None, expert, None),
        P(None, expert, None),
        P(),
        P(),
    )
    return jax.shard_map(
        local, mesh=cut, in_specs=placed, out_specs=P(None, expert, dp), check_vma=False
    )
```

```python
import jax
import jax.numpy as jnp
from jax import lax
from jax.sharding import Mesh
from jax.sharding import PartitionSpec as P

TOPK = 8
CAP = 4
BF = jnp.bfloat16
F32 = jnp.float32

SPLIT = (("p", 2), ("m", 2), ("k", 2), ("zh", 2), ("y", 8), ("x", 4))


def dot(a, b, dims, out=F32):
    return lax.dot_general(a, b, (dims, ((), ())), preferred_element_type=out)


def swap(array, *axes):
    last = 2 ** len(axes) - 1
    return lax.ppermute(array, axes, [(i, last - i) for i in range(last + 1)])


def recut(weight):
    hidden, feats = weight.shape
    k = lax.axis_index("k")
    blocks = weight.reshape(hidden, 2, 2, 2, feats // 8).transpose(3, 2, 0, 1, 4)
    blocks = blocks.reshape(4, hidden, feats // 4)
    blocks = lax.all_to_all(blocks, ("k", "m"), 0, 0, tiled=True)
    blocks = blocks.reshape(2, 2 * hidden, feats // 4)
    own = lax.dynamic_index_in_dim(blocks, k, 0, keepdims=False)
    other = lax.dynamic_index_in_dim(blocks, 1 - k, 0, keepdims=False)
    return own, other


def slots(codes, weights, plan):
    groups, rows = codes.shape
    hosts = plan.shape[0]
    count = hosts // lax.axis_size("zh")
    experts = lax.axis_index("zh") * count + jnp.arange(count, dtype=jnp.int32)
    ids = jnp.arange(hosts, dtype=jnp.int32)
    spare_host = jnp.sum(jnp.where(plan[None, :] == experts[:, None], ids[None, :], 0), axis=1)
    here = jnp.sum(jnp.where(ids[None, :] == experts[:, None], plan[None, :], 0), axis=1)
    own_code = 2 * jnp.concatenate([experts, spare_host])
    spare_code = 2 * jnp.concatenate([here, experts]) + 1
    is_own = codes[:, None, :] == own_code[None, :, None]
    is_spare = codes[:, None, :] == spare_code[None, :, None]
    landed = is_own | is_spare
    at = jnp.arange(rows, dtype=jnp.int32)
    before = (at[:, None] < at[None, :]).astype(BF)
    position = dot(landed.astype(BF), before, ((2,), (0,)))
    fits = position < CAP
    kept = (is_own[:, :count] & fits[:, :count]) | (is_spare[:, count:] & fits[:, count:])
    rank = dot(kept.astype(BF), before, ((2,), (0,)))
    slot = jnp.arange(2 * CAP, dtype=F32)
    hit = kept[:, :, None, :] & (rank[:, :, None, :] == slot[None, None, :, None])
    token = at // TOPK + 1
    tokens_of = jnp.sum(jnp.where(hit, token[None, None, None, :], 0), axis=3)
    group = jnp.arange(groups, dtype=jnp.int32)[:, None, None]
    tokens_of = jnp.where(tokens_of > 0, tokens_of - 1 + group * (rows // TOPK), -1)
    weight_of = jnp.sum(jnp.where(hit, weights[:, None, None, :], 0.0), axis=3)
    order = lambda v: v.transpose(1, 0, 2).reshape(-1)
    return order(tokens_of), order(weight_of)


def both(first, second, axis_name, axis):
    at = lax.axis_index(axis_name)
    return jnp.stack([jnp.where(at == 0, first, second), jnp.where(at == 0, second, first)], axis)


def local(tokens, w_gate, w_down, expert_ids, route_weight, replica_pick, old_plan, new_plan):
    batches, group, feats = tokens.shape
    peers = lax.axis_size("y") * lax.axis_size("x")
    zh, p = lax.axis_index("zh"), lax.axis_index("p")
    code = (2 * expert_ids + (replica_pick & 1)).astype(F32)
    info = jnp.stack([code, route_weight]).reshape(2, batches, group * TOPK)
    info = both(info, swap(info, "zh"), "zh", 2)

    near = both(tokens, swap(tokens, "p"), "p", 2)
    far = both(swap(tokens, "zh"), swap(tokens, "p", "zh"), "p", 2)
    tok = both(near, far, "zh", 1).reshape(batches, 2 * group, 2 * feats)

    gate_own, gate_other = recut(w_gate[0])
    down_own, down_other = recut(w_down[0])

    outputs = []
    for index, plan in ((0, old_plan), (1, new_plan)):
        codes = info[0, index].astype(jnp.int32)
        slot_token, slot_weight = slots(codes, info[1, index], plan)
        pick = slot_token[:, None] == jnp.arange(2 * group, dtype=jnp.int32)[None, :]
        rows = dot(pick.astype(BF), tok[index], ((1,), (0,)), BF)
        rows = rows.reshape(peers, -1, rows.shape[1])
        rows = lax.all_to_all(rows, ("y", "x"), 0, 0, tiled=True).reshape(-1, rows.shape[2])

        send = dot(rows, gate_other, ((1,), (1,)), BF)
        part = dot(rows, gate_own, ((1,), (1,)))
        part = part + swap(send, "k").astype(F32)
        gate = part + swap(part.astype(BF), "m").astype(F32)
        hidden = jax.nn.silu(gate).astype(BF)
        hidden_other = swap(hidden, "k")
        out = dot(hidden, down_own, ((1,), (0,))) + dot(hidden_other, down_other, ((1,), (0,)))
        out = out.astype(BF).reshape(peers, -1, out.shape[1])
        back = lax.all_to_all(out, ("y", "x"), 0, 0, tiled=True).reshape(-1, out.shape[2])

        scale = jnp.where(pick, slot_weight[:, None], 0.0)
        high = scale.astype(BF)
        low = (scale - high.astype(F32)).astype(BF)
        mixed = dot(high, back, ((0,), (0,))) + dot(low, back, ((0,), (0,)))
        mixed = mixed.reshape(2, group, 2, feats)

        def block(other_zh, other_p):
            start = (zh ^ other_zh, 0, p ^ other_p, 0)
            return lax.dynamic_slice(mixed, start, (1, group, 1, feats)).reshape(group, feats)

        total = block(0, 0)
        total = total + swap(block(0, 1).astype(BF), "p").astype(F32)
        total = total + swap(block(1, 0).astype(BF), "zh").astype(F32)
        total = total + swap(block(1, 1).astype(BF), "p", "zh").astype(F32)
        outputs.append(total.astype(BF))
    return jnp.stack(outputs)


def solution(mesh):
    names = tuple(name for name, _ in SPLIT)
    cut = Mesh(mesh.devices.reshape([size for _, size in SPLIT]), names)
    dp, expert = ("p", "m", "k"), ("zh", "y", "x")
    placed = (
        P(None, expert, dp),
        P(expert, dp, None),
        P(expert, dp, None),
        P(None, expert, None),
        P(None, expert, None),
        P(None, expert, None),
        P(),
        P(),
    )
    return jax.shard_map(
        local, mesh=cut, in_specs=placed, out_specs=P(None, expert, dp), check_vma=False
    )
```

```python
import jax
import jax.numpy as jnp
from jax import lax
from jax.sharding import Mesh
from jax.sharding import PartitionSpec as P

TOPK = 8
CAP = 4
BF = jnp.bfloat16
F32 = jnp.float32

SPLIT = (("p", 2), ("m", 2), ("k", 2), ("zh", 2), ("y", 8), ("x", 4))


def dot(a, b, dims, out=F32):
    return lax.dot_general(a, b, (dims, ((), ())), preferred_element_type=out)


def swap(array, *axes):
    last = 2 ** len(axes) - 1
    return lax.ppermute(array, axes, [(i, last - i) for i in range(last + 1)])


def recut(weight):
    hidden, feats = weight.shape
    m, k = lax.axis_index("m"), lax.axis_index("k")
    blocks = weight.reshape(hidden, 2, 2, 2, feats // 8)

    def cut(at_m, at_k):
        start = (0, 0, at_m, at_k, 0)
        return lax.dynamic_slice(blocks, start, (hidden, 2, 1, 1, feats // 8)).reshape(hidden, feats // 4)

    there = swap(jnp.stack([cut(m, 1 - k), cut(1 - m, 1 - k)]), "k")
    near_own, near_other = cut(m, k), there[0]
    far = swap(jnp.stack([cut(1 - m, k), there[1]]), "m")

    def order(near, far):
        first = jnp.where(m == 0, near, far)
        second = jnp.where(m == 0, far, near)
        return jnp.concatenate([first, second], axis=0)

    return order(near_own, far[0]), order(near_other, far[1])


def slots(codes, weights, plan):
    groups, rows = codes.shape
    hosts = plan.shape[0]
    count = hosts // lax.axis_size("zh")
    experts = lax.axis_index("zh") * count + jnp.arange(count, dtype=jnp.int32)
    ids = jnp.arange(hosts, dtype=jnp.int32)
    spare_host = jnp.sum(jnp.where(plan[None, :] == experts[:, None], ids[None, :], 0), axis=1)
    here = jnp.sum(jnp.where(ids[None, :] == experts[:, None], plan[None, :], 0), axis=1)
    own_code = 2 * jnp.concatenate([experts, spare_host])
    spare_code = 2 * jnp.concatenate([here, experts]) + 1
    is_own = codes[:, None, :] == own_code[None, :, None]
    is_spare = codes[:, None, :] == spare_code[None, :, None]
    landed = is_own | is_spare
    at = jnp.arange(rows, dtype=jnp.int32)
    before = (at[:, None] < at[None, :]).astype(BF)
    position = dot(landed.astype(BF), before, ((2,), (0,)))
    fits = position < CAP
    kept = (is_own[:, :count] & fits[:, :count]) | (is_spare[:, count:] & fits[:, count:])
    rank = dot(kept.astype(BF), before, ((2,), (0,)))
    slot = jnp.arange(2 * CAP, dtype=F32)
    hit = kept[:, :, None, :] & (rank[:, :, None, :] == slot[None, None, :, None])
    token = at // TOPK + 1
    tokens_of = jnp.sum(jnp.where(hit, token[None, None, None, :], 0), axis=3)
    group = jnp.arange(groups, dtype=jnp.int32)[:, None, None]
    tokens_of = jnp.where(tokens_of > 0, tokens_of - 1 + group * (rows // TOPK), -1)
    weight_of = jnp.sum(jnp.where(hit, weights[:, None, None, :], 0.0), axis=3)
    order = lambda v: v.transpose(1, 0, 2).reshape(-1)
    return order(tokens_of), order(weight_of)


def thirds(value):
    high = lax.reduce_precision(value, 8, 7)
    mid = lax.reduce_precision(value - high, 8, 7)
    return high.astype(BF), mid.astype(BF), (value - high - mid).astype(BF)


def both(first, second, axis_name, axis):
    at = lax.axis_index(axis_name)
    return jnp.stack([jnp.where(at == 0, first, second), jnp.where(at == 0, second, first)], axis)


def local(tokens, w_gate, w_down, expert_ids, route_weight, replica_pick, old_plan, new_plan):
    batches, group, feats = tokens.shape
    peers = lax.axis_size("y") * lax.axis_size("x")
    zh, p = lax.axis_index("zh"), lax.axis_index("p")
    code = (2 * expert_ids + (replica_pick & 1)).astype(BF)
    parts = [code, *thirds(route_weight)]
    info = jnp.stack(parts).reshape(-1, feats)
    sent = jnp.concatenate([tokens.reshape(-1, feats), jnp.pad(info, ((0, 16 - info.shape[0]), (0, 0)))])
    came = swap(sent, "zh")
    tokens = both(tokens, came[: batches * group].reshape(tokens.shape), "zh", 1)
    tokens = tokens.reshape(batches, 2 * group, feats)
    far_info = came[batches * group :][: info.shape[0]]
    info = both(info, far_info, "zh", 0).reshape(2, 4, batches, group * TOPK).astype(F32)
    code = info[:, 0].astype(jnp.int32)
    weight = info[:, 1] + info[:, 2] + info[:, 3]
    tok = both(tokens, swap(tokens, "p"), "p", 2).reshape(batches, 2 * group, 2 * feats)

    outputs = []
    for index, plan in ((0, old_plan), (1, new_plan)):
        slot_token, slot_weight = slots(code[:, index], weight[:, index], plan)
        pick = slot_token[:, None] == jnp.arange(2 * group, dtype=jnp.int32)[None, :]
        rows = dot(pick.astype(BF), tok[index], ((1,), (0,)), BF)
        rows = rows.reshape(peers, -1, rows.shape[1])
        if index == 0:
            rows, w_gate, w_down = lax.optimization_barrier((rows, w_gate, w_down))
            gate_own, gate_other = recut(w_gate[0])
            down_own, down_other = recut(w_down[0])
        rows = lax.all_to_all(rows, ("y", "x"), 0, 0, tiled=True).reshape(-1, rows.shape[2])

        send = dot(rows, gate_other, ((1,), (1,)), BF)
        part = dot(rows, gate_own, ((1,), (1,)))
        part = part + swap(send, "k").astype(F32)
        gate = part + swap(part.astype(BF), "m").astype(F32)
        hidden = jax.nn.silu(gate).astype(BF)
        hidden_other = swap(hidden, "k")
        out = dot(hidden, down_own, ((1,), (0,))) + dot(hidden_other, down_other, ((1,), (0,)))
        out = out.astype(BF).reshape(peers, -1, out.shape[1])
        back = lax.all_to_all(out, ("y", "x"), 0, 0, tiled=True).reshape(-1, out.shape[2])

        scale = jnp.where(pick, slot_weight[:, None], 0.0)
        high, low, _ = thirds(scale)
        mixed = dot(high, back, ((0,), (0,))) + dot(low, back, ((0,), (0,)))
        mixed = mixed.reshape(2, group, 2, feats)

        def block(other_zh, other_p):
            start = (zh ^ other_zh, 0, p ^ other_p, 0)
            return lax.dynamic_slice(mixed, start, (1, group, 1, feats)).reshape(group, feats)

        total = block(0, 0)
        total = total + swap(block(0, 1).astype(BF), "p").astype(F32)
        total = total + swap(block(1, 0).astype(BF), "zh").astype(F32)
        total = total + swap(block(1, 1).astype(BF), "p", "zh").astype(F32)
        outputs.append(total.astype(BF))
    return jnp.stack(outputs)


def solution(mesh):
    names = tuple(name for name, _ in SPLIT)
    cut = Mesh(mesh.devices.reshape([size for _, size in SPLIT]), names)
    dp, expert = ("p", "m", "k"), ("zh", "y", "x")
    placed = (
        P(None, expert, dp),
        P(expert, dp, None),
        P(expert, dp, None),
        P(None, expert, None),
        P(None, expert, None),
        P(None, expert, None),
        P(),
        P(),
    )
    return jax.shard_map(
        local, mesh=cut, in_specs=placed, out_specs=P(None, expert, dp), check_vma=False
    )
```

```python
import jax
import jax.numpy as jnp
from jax import lax
from jax.experimental import pallas as pl
from jax.experimental.pallas import tpu as pltpu
from jax.sharding import Mesh
from jax.sharding import PartitionSpec as P

TOPK = 8
CAP = 4
BF = jnp.bfloat16
F32 = jnp.float32

SPLIT = (("p", 2), ("m", 2), ("k", 2), ("zh", 2), ("y", 8), ("x", 4))


def dot(a, b, dims, out=F32):
    return lax.dot_general(a, b, (dims, ((), ())), preferred_element_type=out)


def swap(array, *axes):
    last = 2 ** len(axes) - 1
    return lax.ppermute(array, axes, [(i, last - i) for i in range(last + 1)])


def cut_kernel(place, gate, down, *outs):
    m, k = place[0], place[1]
    width = gate.shape[2] // 8
    for which, weight in enumerate((gate, down)):
        for dm in range(2):
            for dk in range(2):
                out = outs[4 * which + 2 * dm + dk]
                for p in range(2):
                    at = (4 * p + 2 * (m ^ dm) + (k ^ dk)) * width
                    out[:, p * width : (p + 1) * width] = weight[0, :, pl.ds(pl.multiple_of(at, width), width)]


def cut_weights(gate, down):
    _, hidden, feats = gate.shape
    place = jnp.stack([lax.axis_index("m"), lax.axis_index("k")]).astype(jnp.int32)
    vmem = pl.BlockSpec(memory_space=pltpu.VMEM)
    parts = pl.pallas_call(
        cut_kernel,
        out_shape=[jax.ShapeDtypeStruct((hidden, feats // 4), BF)] * 8,
        in_specs=[pl.BlockSpec(memory_space=pltpu.SMEM), vmem, vmem],
        out_specs=[vmem] * 8,
        compiler_params=pltpu.CompilerParams(vmem_limit_bytes=32 << 20),
        cost_estimate=pl.CostEstimate(flops=0, bytes_accessed=4 * gate.size * 2, transcendentals=0),
    )(place, gate, down)
    return parts[:4], parts[4:]


def recut(parts):
    m = lax.axis_index("m")
    mine, for_k, for_m, for_mk = parts
    far_own = swap(for_m, "m")
    near_other = swap(for_k, "k")
    far_other = swap(for_mk, "m", "k")

    def order(near, far):
        first = jnp.where(m == 0, near, far)
        second = jnp.where(m == 0, far, near)
        return jnp.concatenate([first, second], axis=0)

    return order(mine, far_own), order(near_other, far_other)


def slots(codes, weights, plan):
    groups, rows = codes.shape
    hosts = plan.shape[0]
    count = hosts // lax.axis_size("zh")
    experts = lax.axis_index("zh") * count + jnp.arange(count, dtype=jnp.int32)
    ids = jnp.arange(hosts, dtype=jnp.int32)
    spare_host = jnp.sum(jnp.where(plan[None, :] == experts[:, None], ids[None, :], 0), axis=1)
    here = jnp.sum(jnp.where(ids[None, :] == experts[:, None], plan[None, :], 0), axis=1)
    own_code = 2 * jnp.concatenate([experts, spare_host])
    spare_code = 2 * jnp.concatenate([here, experts]) + 1
    is_own = codes[:, None, :] == own_code[None, :, None]
    is_spare = codes[:, None, :] == spare_code[None, :, None]
    landed = is_own | is_spare
    at = jnp.arange(rows, dtype=jnp.int32)
    before = (at[:, None] < at[None, :]).astype(BF)
    position = dot(landed.astype(BF), before, ((2,), (0,)))
    fits = position < CAP
    kept = (is_own[:, :count] & fits[:, :count]) | (is_spare[:, count:] & fits[:, count:])
    rank = dot(kept.astype(BF), before, ((2,), (0,)))
    slot = jnp.arange(2 * CAP, dtype=F32)
    hit = kept[:, :, None, :] & (rank[:, :, None, :] == slot[None, None, :, None])
    token = at // TOPK + 1
    tokens_of = jnp.sum(jnp.where(hit, token[None, None, None, :], 0), axis=3)
    group = jnp.arange(groups, dtype=jnp.int32)[:, None, None]
    tokens_of = jnp.where(tokens_of > 0, tokens_of - 1 + group * (rows // TOPK), -1)
    weight_of = jnp.sum(jnp.where(hit, weights[:, None, None, :], 0.0), axis=3)
    order = lambda v: v.transpose(1, 0, 2).reshape(-1)
    return order(tokens_of), order(weight_of)


def thirds(value):
    high = lax.reduce_precision(value, 8, 7)
    mid = lax.reduce_precision(value - high, 8, 7)
    return high.astype(BF), mid.astype(BF), (value - high - mid).astype(BF)


def local(tokens, w_gate, w_down, expert_ids, route_weight, replica_pick, old_plan, new_plan):
    batches, group, feats = tokens.shape
    peers = lax.axis_size("y") * lax.axis_size("x")
    code = (2 * expert_ids + (replica_pick & 1)).astype(BF)
    parts = [code, *thirds(route_weight)]
    info = jnp.stack(parts).reshape(-1, feats)
    count = info.shape[0]
    sent = jnp.concatenate([tokens.reshape(-1, feats), jnp.pad(info, ((0, 16 - count), (0, 0)))])
    sent = jnp.broadcast_to(sent[None], (4, *sent.shape))
    came = lax.all_to_all(sent, ("p", "zh"), 0, 0, tiled=True).reshape(2, 2, -1, feats)
    tok = came[:, :, : batches * group].reshape(2, 2, batches, group, feats)
    tok = tok.transpose(2, 1, 3, 0, 4).reshape(batches, 2 * group, 2 * feats)
    info = came[0, :, batches * group : batches * group + count]
    info = info.reshape(2, 4, batches, group * TOPK).astype(F32)
    code = info[:, 0].astype(jnp.int32)
    weight = info[:, 1] + info[:, 2] + info[:, 3]

    gate_parts, down_parts = cut_weights(w_gate, w_down)
    outputs = []
    for index, plan in ((0, old_plan), (1, new_plan)):
        slot_token, slot_weight = slots(code[:, index], weight[:, index], plan)
        pick = slot_token[:, None] == jnp.arange(2 * group, dtype=jnp.int32)[None, :]
        rows = dot(pick.astype(BF), tok[index], ((1,), (0,)), BF)
        rows = rows.reshape(peers, -1, rows.shape[1])
        if index == 0:
            rows, gate_parts, down_parts = lax.optimization_barrier((rows, gate_parts, down_parts))
            gate_own, gate_other = recut(gate_parts)
            down_own, down_other = recut(down_parts)
        rows = lax.all_to_all(rows, ("y", "x"), 0, 0, tiled=True).reshape(-1, rows.shape[2])

        send = dot(rows, gate_other, ((1,), (1,)), BF)
        part = dot(rows, gate_own, ((1,), (1,)))
        part = part + swap(send, "k").astype(F32)
        gate = part + swap(part.astype(BF), "m").astype(F32)
        hidden = jax.nn.silu(gate).astype(BF)
        hidden_other = swap(hidden, "k")
        out = dot(hidden, down_own, ((1,), (0,))) + dot(hidden_other, down_other, ((1,), (0,)))
        out = out.astype(BF).reshape(peers, -1, out.shape[1])
        back = lax.all_to_all(out, ("y", "x"), 0, 0, tiled=True).reshape(-1, out.shape[2])

        scale = jnp.where(pick, slot_weight[:, None], 0.0)
        high, low, _ = thirds(scale)
        mixed = dot(high, back, ((0,), (0,))) + dot(low, back, ((0,), (0,)))
        outputs.append(mixed.astype(BF).reshape(2, group, 2, feats))
    mixed = jnp.stack(outputs).transpose(3, 1, 0, 2, 4).reshape(4, batches * group, feats)
    terms = lax.all_to_all(mixed, ("p", "zh"), 0, 0, tiled=True)
    return jnp.sum(terms.astype(F32), axis=0).astype(BF).reshape(batches, group, feats)


def solution(mesh):
    names = tuple(name for name, _ in SPLIT)
    cut = Mesh(mesh.devices.reshape([size for _, size in SPLIT]), names)
    dp, expert = ("p", "m", "k"), ("zh", "y", "x")
    placed = (
        P(None, expert, dp),
        P(expert, dp, None),
        P(expert, dp, None),
        P(None, expert, None),
        P(None, expert, None),
        P(None, expert, None),
        P(),
        P(),
    )
    return jax.shard_map(
        local, mesh=cut, in_specs=placed, out_specs=P(None, expert, dp), check_vma=False
    )
```

```python
import jax
import jax.numpy as jnp
from jax import lax
from jax.experimental import pallas as pl
from jax.experimental.pallas import tpu as pltpu
from jax.sharding import Mesh
from jax.sharding import PartitionSpec as P

TOPK = 8
CAP = 4
BF = jnp.bfloat16
F32 = jnp.float32

SPLIT = (("p", 2), ("m", 2), ("k", 2), ("zh", 2), ("y", 8), ("x", 4))


def dot(a, b, dims, out=F32):
    return lax.dot_general(a, b, (dims, ((), ())), preferred_element_type=out)


def swap(array, *axes):
    last = 2 ** len(axes) - 1
    return lax.ppermute(array, axes, [(i, last - i) for i in range(last + 1)])


def cut_kernel(place, gate, down, *outs):
    m, k = place[0], place[1]
    width = gate.shape[2] // 8
    for which, weight in enumerate((gate, down)):
        for dm in range(2):
            for dk in range(2):
                out = outs[4 * which + 2 * dm + dk]
                for p in range(2):
                    at = (4 * p + 2 * (m ^ dm) + (k ^ dk)) * width
                    out[:, p * width : (p + 1) * width] = weight[0, :, pl.ds(pl.multiple_of(at, width), width)]


def cut_weights(gate, down):
    _, hidden, feats = gate.shape
    place = jnp.stack([lax.axis_index("m"), lax.axis_index("k")]).astype(jnp.int32)
    rows = hidden // 2
    whole = pl.BlockSpec((1, rows, feats), lambda i: (0, i, 0))
    parts = pl.pallas_call(
        cut_kernel,
        out_shape=[jax.ShapeDtypeStruct((hidden, feats // 4), BF)] * 8,
        grid=(2,),
        in_specs=[pl.BlockSpec(memory_space=pltpu.SMEM), whole, whole],
        out_specs=[pl.BlockSpec((rows, feats // 4), lambda i: (i, 0))] * 8,
        compiler_params=pltpu.CompilerParams(vmem_limit_bytes=32 << 20),
        cost_estimate=pl.CostEstimate(flops=0, bytes_accessed=4 * gate.size * 2, transcendentals=0),
    )(place, gate, down)
    return parts[:4], parts[4:]


def recut(parts):
    m = lax.axis_index("m")
    mine, for_k, for_m, for_mk = parts
    far_own = swap(for_m, "m")
    near_other = swap(for_k, "k")
    far_other = swap(for_mk, "m", "k")

    def order(near, far):
        first = jnp.where(m == 0, near, far)
        second = jnp.where(m == 0, far, near)
        return jnp.concatenate([first, second], axis=0)

    return order(mine, far_own), order(near_other, far_other)


def thirds(value):
    high = lax.reduce_precision(value, 8, 7)
    mid = lax.reduce_precision(value - high, 8, 7)
    return high.astype(BF), mid.astype(BF), (value - high - mid).astype(BF)


def slots(codes, weights, plan, experts):
    rows = codes.shape[1]
    count = experts.shape[0]
    ids = jnp.arange(plan.shape[0], dtype=jnp.int32)
    spare_host = jnp.sum(jnp.where(plan[None, :] == experts[:, None], ids[None, :], 0), axis=1)
    here = jnp.sum(jnp.where(ids[None, :] == experts[:, None], plan[None, :], 0), axis=1)
    own_code = 2 * jnp.concatenate([experts, spare_host])
    spare_code = 2 * jnp.concatenate([here, experts]) + 1
    is_own = codes[:, None, :] == own_code[None, :, None]
    is_spare = codes[:, None, :] == spare_code[None, :, None]
    landed = is_own | is_spare
    at = jnp.arange(rows, dtype=jnp.int32)
    before = (at[:, None] < at[None, :]).astype(BF)
    position = dot(landed.astype(BF), before, ((2,), (0,)))
    fits = position < CAP
    kept = (is_own[:, :count] & fits[:, :count]) | (is_spare[:, count:] & fits[:, count:])
    rank = dot(kept.astype(BF), before, ((2,), (0,)))
    slot = jnp.arange(2 * CAP, dtype=F32)
    hit = kept[:, :, None, :] & (rank[:, :, None, :] == slot[None, None, :, None])
    token = at // TOPK + 1
    token_of = jnp.sum(jnp.where(hit, token[None, None, None, :], 0), axis=3) - 1
    weight_of = jnp.sum(jnp.where(hit, weights[:, None, None, :], 0.0), axis=3)
    return token_of, weight_of


def placed(token_of, starts, total):
    at = jnp.where(token_of >= 0, token_of + starts[:, None, None], -1)
    at = at.transpose(1, 0, 2).reshape(-1)
    return at[:, None] == jnp.arange(total, dtype=jnp.int32)[None, :]


def combine(hot, weight_of, back):
    scale = jnp.where(hot, weight_of.transpose(1, 0, 2).reshape(-1)[:, None], 0.0)
    high, low, _ = thirds(scale)
    return (dot(high, back, ((0,), (0,))) + dot(low, back, ((0,), (0,)))).astype(BF)


def local(tokens, w_gate, w_down, expert_ids, route_weight, replica_pick, old_plan, new_plan):
    batches, group, feats = tokens.shape
    ny, nx, wide = lax.axis_size("y"), lax.axis_size("x"), 2 * feats
    zh, y = lax.axis_index("zh"), lax.axis_index("y")
    gate_parts, down_parts = cut_weights(w_gate, w_down)
    gate_own, gate_other = recut(gate_parts)
    down_own, down_other = recut(down_parts)

    code = (2 * expert_ids + (replica_pick & 1)).astype(BF)
    info = jnp.stack([code, *thirds(route_weight)]).reshape(-1, feats)
    count = info.shape[0]
    sent = jnp.concatenate([tokens.reshape(-1, feats), jnp.pad(info, ((0, 16 - count), (0, 0)))])
    sent = jnp.broadcast_to(sent[None], (4, *sent.shape))
    came = lax.all_to_all(sent, ("p", "zh"), 0, 0, tiled=True).reshape(2, 2, -1, feats)
    tok = came[:, :, : batches * group].reshape(2, 2, batches, group, feats)
    tok = tok.transpose(2, 1, 3, 0, 4).reshape(batches, 2 * group, wide)
    info = came[0, :, batches * group : batches * group + count]

    def unpack(info, groups):
        info = info.reshape(groups, 4, batches, group * TOPK).astype(F32)
        return info[:, 0].astype(jnp.int32), info[:, 1] + info[:, 2] + info[:, 3]

    lines = info.reshape(-1, wide)
    step = 2 * group + 8
    lines = jnp.pad(lines, ((0, 8 - lines.shape[0]), (0, 0)))
    spread = lax.all_gather(jnp.concatenate([tok[1], lines]), "y", axis=0, tiled=True)

    near_code, near_weight = unpack(info, 2)
    near_experts = zh * (ny * nx) + jnp.arange(ny * nx, dtype=jnp.int32)
    near_starts = jnp.arange(2, dtype=jnp.int32) * group

    def near_slots(index, plan):
        token_of, weight_of = slots(near_code[:, index], near_weight[:, index], plan, near_experts)
        return placed(token_of, near_starts, 2 * group), weight_of

    row_experts = (zh * ny + y) * nx + jnp.arange(nx, dtype=jnp.int32)
    at = jnp.arange(2 * ny, dtype=jnp.int32)
    starts = (at // 2) * step + (at % 2) * group
    flat_starts = at * group

    def experts_out(rows):
        send = dot(rows, gate_other, ((1,), (1,)), BF)
        part = dot(rows, gate_own, ((1,), (1,)))
        part = part + swap(send, "k").astype(F32)
        gate = part + swap(part.astype(BF), "m").astype(F32)
        hidden = jax.nn.silu(gate).astype(BF)
        hidden_other = swap(hidden, "k")
        out = dot(hidden, down_own, ((1,), (0,))) + dot(hidden_other, down_other, ((1,), (0,)))
        return out.astype(BF)

    hot, _ = near_slots(0, old_plan)
    rows = dot(hot.astype(BF), tok[0], ((1,), (0,)), BF).reshape(ny * nx, -1, wide)
    rows = lax.all_to_all(rows, ("y", "x"), 0, 0, tiled=True).reshape(-1, wide)
    out_0 = experts_out(rows)

    all_code, all_weight = unpack(spread.reshape(ny, step, wide)[:, 2 * group : step - 4], 2 * ny)
    token_of, _ = slots(all_code[:, 1], all_weight[:, 1], new_plan, row_experts)
    hot = placed(token_of, starts, ny * step)
    rows = dot(hot.astype(BF), spread, ((1,), (0,)), BF).reshape(nx, -1, wide)
    rows = lax.all_to_all(rows, "x", 0, 0, tiled=True).reshape(-1, wide)
    out_1 = experts_out(rows)

    back = out_0.reshape(ny, nx, -1, wide).transpose(1, 0, 2, 3).reshape(nx, -1, wide)
    back = lax.all_to_all(back, "x", 0, 0, tiled=True).reshape(-1, wide)
    token_of, weight_of = slots(all_code[:, 0], all_weight[:, 0], old_plan, row_experts)
    mixed_0 = combine(placed(token_of, flat_starts, 2 * ny * group), weight_of, back)
    mixed_0 = lax.psum_scatter(mixed_0, "y", scatter_dimension=0, tiled=True)

    back = out_1.reshape(nx, ny, -1, wide).transpose(1, 0, 2, 3).reshape(ny * nx, -1, wide)
    back = lax.all_to_all(back, ("y", "x"), 0, 0, tiled=True).reshape(-1, wide)
    hot, weight_of = near_slots(1, new_plan)
    mixed_1 = combine(hot, weight_of, back)

    mixed = jnp.stack([mixed_0, mixed_1]).reshape(batches, 2, group, 2, feats)
    mixed = mixed.transpose(3, 1, 0, 2, 4).reshape(4, batches * group, feats)
    terms = lax.all_to_all(mixed, ("p", "zh"), 0, 0, tiled=True)
    return jnp.sum(terms.astype(F32), axis=0).astype(BF).reshape(batches, group, feats)


def solution(mesh):
    names = tuple(name for name, _ in SPLIT)
    cut = Mesh(mesh.devices.reshape([size for _, size in SPLIT]), names)
    dp, expert = ("p", "m", "k"), ("zh", "y", "x")
    specs = (
        P(None, expert, dp),
        P(expert, dp, None),
        P(expert, dp, None),
        P(None, expert, None),
        P(None, expert, None),
        P(None, expert, None),
        P(),
        P(),
    )
    return jax.shard_map(
        local, mesh=cut, in_specs=specs, out_specs=P(None, expert, dp), check_vma=False
    )
```

```python
import jax
import jax.numpy as jnp
from jax import lax
from jax.experimental import pallas as pl
from jax.experimental.pallas import tpu as pltpu
from jax.sharding import Mesh
from jax.sharding import PartitionSpec as P

TOPK = 8
CAP = 4
BF = jnp.bfloat16
F32 = jnp.float32

SPLIT = (("p", 2), ("m", 2), ("k", 2), ("zh", 2), ("y", 8), ("x", 4))


def dot(a, b, dims, out=F32):
    return lax.dot_general(a, b, (dims, ((), ())), preferred_element_type=out)


def swap(array, *axes):
    last = 2 ** len(axes) - 1
    return lax.ppermute(array, axes, [(i, last - i) for i in range(last + 1)])


def cut_kernel(place, gate, down, *outs):
    m, k = place[0], place[1]
    width = gate.shape[2] // 8
    for which, weight in enumerate((gate, down)):
        for dm in range(2):
            for dk in range(2):
                out = outs[4 * which + 2 * dm + dk]
                for p in range(2):
                    at = (4 * p + 2 * (m ^ dm) + (k ^ dk)) * width
                    out[:, p * width : (p + 1) * width] = weight[0, :, pl.ds(pl.multiple_of(at, width), width)]


def cut_weights(gate, down):
    _, hidden, feats = gate.shape
    place = jnp.stack([lax.axis_index("m"), lax.axis_index("k")]).astype(jnp.int32)
    rows = hidden // 2
    whole = pl.BlockSpec((1, rows, feats), lambda i: (0, i, 0))
    parts = pl.pallas_call(
        cut_kernel,
        out_shape=[jax.ShapeDtypeStruct((hidden, feats // 4), BF)] * 8,
        grid=(2,),
        in_specs=[pl.BlockSpec(memory_space=pltpu.SMEM), whole, whole],
        out_specs=[pl.BlockSpec((rows, feats // 4), lambda i: (i, 0))] * 8,
        compiler_params=pltpu.CompilerParams(vmem_limit_bytes=32 << 20),
        cost_estimate=pl.CostEstimate(flops=0, bytes_accessed=4 * gate.size * 2, transcendentals=0),
    )(place, gate, down)
    return parts[:4], parts[4:]


def recut(parts):
    m = lax.axis_index("m")
    mine, for_k, for_m, for_mk = parts
    far_own = swap(for_m, "m")
    near_other = swap(for_k, "k")
    far_other = swap(for_mk, "m", "k")

    def order(near, far):
        first = jnp.where(m == 0, near, far)
        second = jnp.where(m == 0, far, near)
        return jnp.concatenate([first, second], axis=0)

    return order(mine, far_own), order(near_other, far_other)


def slots(codes, weights, plan):
    groups, rows = codes.shape
    hosts = plan.shape[0]
    count = hosts // lax.axis_size("zh")
    experts = lax.axis_index("zh") * count + jnp.arange(count, dtype=jnp.int32)
    ids = jnp.arange(hosts, dtype=jnp.int32)
    spare_host = jnp.sum(jnp.where(plan[None, :] == experts[:, None], ids[None, :], 0), axis=1)
    here = jnp.sum(jnp.where(ids[None, :] == experts[:, None], plan[None, :], 0), axis=1)
    own_code = 2 * jnp.concatenate([experts, spare_host])
    spare_code = 2 * jnp.concatenate([here, experts]) + 1
    is_own = codes[:, None, :] == own_code[None, :, None]
    is_spare = codes[:, None, :] == spare_code[None, :, None]
    landed = is_own | is_spare
    at = jnp.arange(rows, dtype=jnp.int32)
    before = (at[:, None] < at[None, :]).astype(BF)
    position = dot(landed.astype(BF), before, ((2,), (0,)))
    fits = position < CAP
    kept = (is_own[:, :count] & fits[:, :count]) | (is_spare[:, count:] & fits[:, count:])
    rank = dot(kept.astype(BF), before, ((2,), (0,)))
    slot = jnp.arange(2 * CAP, dtype=F32)
    hit = kept[:, :, None, :] & (rank[:, :, None, :] == slot[None, None, :, None])
    token = at // TOPK + 1
    tokens_of = jnp.sum(jnp.where(hit, token[None, None, None, :], 0), axis=3)
    group = jnp.arange(groups, dtype=jnp.int32)[:, None, None]
    tokens_of = jnp.where(tokens_of > 0, tokens_of - 1 + group * (rows // TOPK), -1)
    weight_of = jnp.sum(jnp.where(hit, weights[:, None, None, :], 0.0), axis=3)
    order = lambda v: v.transpose(1, 0, 2).reshape(-1)
    return order(tokens_of), order(weight_of)


def thirds(value):
    high = lax.reduce_precision(value, 8, 7)
    mid = lax.reduce_precision(value - high, 8, 7)
    return high.astype(BF), mid.astype(BF), (value - high - mid).astype(BF)


def local(tokens, w_gate, w_down, expert_ids, route_weight, replica_pick, old_plan, new_plan):
    batches, group, feats = tokens.shape
    peers = lax.axis_size("y") * lax.axis_size("x")
    code = (2 * expert_ids + (replica_pick & 1)).astype(BF)
    parts = [code, *thirds(route_weight)]
    info = jnp.stack(parts).reshape(-1, feats)
    count = info.shape[0]
    sent = jnp.concatenate([tokens.reshape(-1, feats), jnp.pad(info, ((0, 16 - count), (0, 0)))])
    sent = jnp.broadcast_to(sent[None], (4, *sent.shape))
    came = lax.all_to_all(sent, ("p", "zh"), 0, 0, tiled=True).reshape(2, 2, -1, feats)
    tok = came[:, :, : batches * group].reshape(2, 2, batches, group, feats)
    tok = tok.transpose(2, 1, 3, 0, 4).reshape(batches, 2 * group, 2 * feats)
    info = came[0, :, batches * group : batches * group + count]
    info = info.reshape(2, 4, batches, group * TOPK).astype(F32)
    code = info[:, 0].astype(jnp.int32)
    weight = info[:, 1] + info[:, 2] + info[:, 3]

    gate_parts, down_parts = cut_weights(w_gate, w_down)
    gate_own, gate_other = recut(gate_parts)
    down_own, down_other = recut(down_parts)
    outputs = []
    for index, plan in ((0, old_plan), (1, new_plan)):
        slot_token, slot_weight = slots(code[:, index], weight[:, index], plan)
        pick = slot_token[:, None] == jnp.arange(2 * group, dtype=jnp.int32)[None, :]
        rows = dot(pick.astype(BF), tok[index], ((1,), (0,)), BF)
        rows = rows.reshape(peers, -1, rows.shape[1])
        rows = lax.all_to_all(rows, ("y", "x"), 0, 0, tiled=True).reshape(-1, rows.shape[2])

        send = dot(rows, gate_other, ((1,), (1,)), BF)
        part = dot(rows, gate_own, ((1,), (1,)))
        part = part + swap(send, "k").astype(F32)
        gate = part + swap(part.astype(BF), "m").astype(F32)
        hidden = jax.nn.silu(gate).astype(BF)
        hidden_other = swap(hidden, "k")
        out = dot(hidden, down_own, ((1,), (0,))) + dot(hidden_other, down_other, ((1,), (0,)))
        out = out.astype(BF).reshape(peers, -1, out.shape[1])
        back = lax.all_to_all(out, ("y", "x"), 0, 0, tiled=True).reshape(-1, out.shape[2])

        scale = jnp.where(pick, slot_weight[:, None], 0.0)
        high, low, _ = thirds(scale)
        mixed = dot(high, back, ((0,), (0,))) + dot(low, back, ((0,), (0,)))
        outputs.append(mixed.astype(BF).reshape(2, group, 2, feats))
    mixed = jnp.stack(outputs).transpose(3, 1, 0, 2, 4).reshape(4, batches * group, feats)
    terms = lax.all_to_all(mixed, ("p", "zh"), 0, 0, tiled=True)
    return jnp.sum(terms.astype(F32), axis=0).astype(BF).reshape(batches, group, feats)


def solution(mesh):
    names = tuple(name for name, _ in SPLIT)
    cut = Mesh(mesh.devices.reshape([size for _, size in SPLIT]), names)
    dp, expert = ("p", "m", "k"), ("zh", "y", "x")
    placed = (
        P(None, expert, dp),
        P(expert, dp, None),
        P(expert, dp, None),
        P(None, expert, None),
        P(None, expert, None),
        P(None, expert, None),
        P(),
        P(),
    )
    return jax.shard_map(
        local, mesh=cut, in_specs=placed, out_specs=P(None, expert, dp), check_vma=False
    )
```

```python
import jax
import jax.numpy as jnp
from jax import lax
from jax.experimental import pallas as pl
from jax.experimental.pallas import tpu as pltpu
from jax.sharding import Mesh
from jax.sharding import PartitionSpec as P

TOPK = 8
CAP = 4
BF = jnp.bfloat16
F32 = jnp.float32

SPLIT = (("p", 2), ("m", 2), ("k", 2), ("zh", 2), ("y", 8), ("x", 4))


def dot(a, b, dims, out=F32):
    return lax.dot_general(a, b, (dims, ((), ())), preferred_element_type=out)


def swap(array, *axes):
    last = 2 ** len(axes) - 1
    return lax.ppermute(array, axes, [(i, last - i) for i in range(last + 1)])


def cut_kernel(place, gate, down, *outs):
    m, k = place[0], place[1]
    width = gate.shape[2] // 8
    for which, weight in enumerate((gate, down)):
        mine, for_k, for_m = outs[3 * which : 3 * which + 3]
        for dm, dk, out in ((0, 0, mine), (0, 1, for_k), (1, 0, for_m.at[0]), (1, 1, for_m.at[1])):
            for p in range(2):
                at = (4 * p + 2 * (m ^ dm) + (k ^ dk)) * width
                out[:, p * width : (p + 1) * width] = weight[0, :, pl.ds(pl.multiple_of(at, width), width)]


def cut_weights(gate, down):
    _, hidden, feats = gate.shape
    place = jnp.stack([lax.axis_index("m"), lax.axis_index("k")]).astype(jnp.int32)
    rows = hidden // 2
    whole = pl.BlockSpec((1, rows, feats), lambda i: (0, i, 0))
    one = pl.BlockSpec((rows, feats // 4), lambda i: (i, 0))
    two = pl.BlockSpec((2, rows, feats // 4), lambda i: (0, i, 0))
    shape = lambda *lead: jax.ShapeDtypeStruct((*lead, hidden, feats // 4), BF)
    parts = pl.pallas_call(
        cut_kernel,
        out_shape=[shape(), shape(), shape(2)] * 2,
        grid=(2,),
        in_specs=[pl.BlockSpec(memory_space=pltpu.SMEM), whole, whole],
        out_specs=[one, one, two] * 2,
        compiler_params=pltpu.CompilerParams(vmem_limit_bytes=32 << 20),
        cost_estimate=pl.CostEstimate(flops=0, bytes_accessed=4 * gate.size * 2, transcendentals=0),
    )(place, gate, down)
    return parts[:3], parts[3:]


def order(near, far):
    m = lax.axis_index("m")
    first = jnp.where(m == 0, near, far)
    second = jnp.where(m == 0, far, near)
    return jnp.concatenate([first, second], axis=0)


def slots(codes, weights, plan):
    groups, rows = codes.shape
    hosts = plan.shape[0]
    count = hosts // lax.axis_size("zh")
    experts = lax.axis_index("zh") * count + jnp.arange(count, dtype=jnp.int32)
    ids = jnp.arange(hosts, dtype=jnp.int32)
    spare_host = jnp.sum(jnp.where(plan[None, :] == experts[:, None], ids[None, :], 0), axis=1)
    here = jnp.sum(jnp.where(ids[None, :] == experts[:, None], plan[None, :], 0), axis=1)
    own_code = 2 * jnp.concatenate([experts, spare_host])
    spare_code = 2 * jnp.concatenate([here, experts]) + 1
    is_own = codes[:, None, :] == own_code[None, :, None]
    is_spare = codes[:, None, :] == spare_code[None, :, None]
    landed = is_own | is_spare
    at = jnp.arange(rows, dtype=jnp.int32)
    before = (at[:, None] < at[None, :]).astype(BF)
    position = dot(landed.astype(BF), before, ((2,), (0,)))
    fits = position < CAP
    kept = (is_own[:, :count] & fits[:, :count]) | (is_spare[:, count:] & fits[:, count:])
    rank = dot(kept.astype(BF), before, ((2,), (0,)))
    slot = jnp.arange(2 * CAP, dtype=F32)
    hit = kept[:, :, None, :] & (rank[:, :, None, :] == slot[None, None, :, None])
    token = at // TOPK + 1
    tokens_of = jnp.sum(jnp.where(hit, token[None, None, None, :], 0), axis=3)
    group = jnp.arange(groups, dtype=jnp.int32)[:, None, None]
    tokens_of = jnp.where(tokens_of > 0, tokens_of - 1 + group * (rows // TOPK), -1)
    weight_of = jnp.sum(jnp.where(hit, weights[:, None, None, :], 0.0), axis=3)
    order = lambda v: v.transpose(1, 0, 2).reshape(-1)
    return order(tokens_of), order(weight_of)


def thirds(value):
    high = lax.reduce_precision(value, 8, 7)
    mid = lax.reduce_precision(value - high, 8, 7)
    return high.astype(BF), mid.astype(BF), (value - high - mid).astype(BF)


def local(tokens, w_gate, w_down, expert_ids, route_weight, replica_pick, old_plan, new_plan):
    batches, group, feats = tokens.shape
    peers = lax.axis_size("y") * lax.axis_size("x")
    code = (2 * expert_ids + (replica_pick & 1)).astype(BF)
    parts = [code, *thirds(route_weight)]
    info = jnp.stack(parts).reshape(-1, feats)
    count = info.shape[0]
    sent = jnp.concatenate([tokens.reshape(-1, feats), jnp.pad(info, ((0, 16 - count), (0, 0)))])
    sent = jnp.broadcast_to(sent[None], (4, *sent.shape))
    came = lax.all_to_all(sent, ("p", "zh"), 0, 0, tiled=True).reshape(2, 2, -1, feats)
    tok = came[:, :, : batches * group].reshape(2, 2, batches, group, feats)
    tok = tok.transpose(2, 1, 3, 0, 4).reshape(batches, 2 * group, 2 * feats)
    info = came[0, :, batches * group : batches * group + count]
    info = info.reshape(2, 4, batches, group * TOPK).astype(F32)
    code = info[:, 0].astype(jnp.int32)
    weight = info[:, 1] + info[:, 2] + info[:, 3]

    gate_parts, down_parts = cut_weights(w_gate, w_down)
    gate_far = swap(gate_parts[2], "m")

    outputs = []
    for index, plan in ((0, old_plan), (1, new_plan)):
        slot_token, slot_weight = slots(code[:, index], weight[:, index], plan)
        pick = slot_token[:, None] == jnp.arange(2 * group, dtype=jnp.int32)[None, :]
        rows = dot(pick.astype(BF), tok[index], ((1,), (0,)), BF)
        rows = rows.reshape(peers, -1, rows.shape[1])
        if index == 0:
            rows, gate_far, down_ready = lax.optimization_barrier((rows, gate_far, down_parts[2]))
            down_far = swap(down_ready, "m")
            gate_own = order(gate_parts[0], gate_far[0])
            gate_other = swap(order(gate_parts[1], gate_far[1]), "k")
            down_own = order(down_parts[0], down_far[0])
            down_other = swap(order(down_parts[1], down_far[1]), "k")
        else:
            rows, gate_other, down_other = lax.optimization_barrier((rows, gate_other, down_other))
        rows = lax.all_to_all(rows, ("y", "x"), 0, 0, tiled=True).reshape(-1, rows.shape[2])

        send = dot(rows, gate_other, ((1,), (1,)), BF)
        part = dot(rows, gate_own, ((1,), (1,)))
        part = part + swap(send, "k").astype(F32)
        gate = part + swap(part.astype(BF), "m").astype(F32)
        hidden = jax.nn.silu(gate).astype(BF)
        hidden_other = swap(hidden, "k")
        out = dot(hidden, down_own, ((1,), (0,))) + dot(hidden_other, down_other, ((1,), (0,)))
        out = out.astype(BF).reshape(peers, -1, out.shape[1])
        back = lax.all_to_all(out, ("y", "x"), 0, 0, tiled=True).reshape(-1, out.shape[2])

        scale = jnp.where(pick, slot_weight[:, None], 0.0)
        high, low, _ = thirds(scale)
        mixed = dot(high, back, ((0,), (0,))) + dot(low, back, ((0,), (0,)))
        outputs.append(mixed.astype(BF).reshape(2, group, 2, feats))
    mixed = jnp.stack(outputs).transpose(3, 1, 0, 2, 4).reshape(4, batches * group, feats)
    terms = lax.all_to_all(mixed, ("p", "zh"), 0, 0, tiled=True)
    return jnp.sum(terms.astype(F32), axis=0).astype(BF).reshape(batches, group, feats)


def solution(mesh):
    names = tuple(name for name, _ in SPLIT)
    cut = Mesh(mesh.devices.reshape([size for _, size in SPLIT]), names)
    dp, expert = ("p", "m", "k"), ("zh", "y", "x")
    placed = (
        P(None, expert, dp),
        P(expert, dp, None),
        P(expert, dp, None),
        P(None, expert, None),
        P(None, expert, None),
        P(None, expert, None),
        P(),
        P(),
    )
    return jax.shard_map(
        local, mesh=cut, in_specs=placed, out_specs=P(None, expert, dp), check_vma=False
    )
```

```python
import functools

import jax
import jax.numpy as jnp
from jax import lax
from jax.experimental import pallas as pl
from jax.experimental.pallas import tpu as pltpu
from jax.sharding import Mesh
from jax.sharding import PartitionSpec as P

TOPK = 8
CAP = 4
BF = jnp.bfloat16
F32 = jnp.float32

SPLIT = (("p", 2), ("m", 2), ("k", 2), ("zh", 2), ("y", 8), ("x", 4))


def dot(a, b, dims, out=F32):
    return lax.dot_general(a, b, (dims, ((), ())), preferred_element_type=out)


def swap(array, *axes):
    last = 2 ** len(axes) - 1
    return lax.ppermute(array, axes, [(i, last - i) for i in range(last + 1)])


def cut_kernel(place, gate, down, *outs):
    m, k = place[0], place[1]
    width = gate.shape[2] // 8
    for which, weight in enumerate((gate, down)):
        mine, for_k, for_m = outs[3 * which : 3 * which + 3]
        for dm, dk, out in ((0, 0, mine), (0, 1, for_k), (1, 0, for_m.at[0]), (1, 1, for_m.at[1])):
            for p in range(2):
                at = (4 * p + 2 * (m ^ dm) + (k ^ dk)) * width
                out[:, p * width : (p + 1) * width] = weight[0, :, pl.ds(pl.multiple_of(at, width), width)]


def cut_weights(gate, down):
    _, hidden, feats = gate.shape
    place = jnp.stack([lax.axis_index("m"), lax.axis_index("k")]).astype(jnp.int32)
    rows = hidden // 2
    whole = pl.BlockSpec((1, rows, feats), lambda i: (0, i, 0))
    one = pl.BlockSpec((rows, feats // 4), lambda i: (i, 0))
    two = pl.BlockSpec((2, rows, feats // 4), lambda i: (0, i, 0))
    shape = lambda *lead: jax.ShapeDtypeStruct((*lead, hidden, feats // 4), BF)
    parts = pl.pallas_call(
        cut_kernel,
        out_shape=[shape(), shape(), shape(2)] * 2,
        grid=(2,),
        in_specs=[pl.BlockSpec(memory_space=pltpu.SMEM), whole, whole],
        out_specs=[one, one, two] * 2,
        compiler_params=pltpu.CompilerParams(vmem_limit_bytes=32 << 20),
        cost_estimate=pl.CostEstimate(flops=0, bytes_accessed=4 * gate.size * 2, transcendentals=0),
    )(place, gate, down)
    return parts[:3], parts[3:]


def order(near, far):
    m = lax.axis_index("m")
    first = jnp.where(m == 0, near, far)
    second = jnp.where(m == 0, far, near)
    return jnp.concatenate([first, second], axis=0)


def slots(codes, weights, plan):
    groups, rows = codes.shape
    hosts = plan.shape[0]
    count = hosts // lax.axis_size("zh")
    experts = lax.axis_index("zh") * count + jnp.arange(count, dtype=jnp.int32)
    ids = jnp.arange(hosts, dtype=jnp.int32)
    spare_host = jnp.sum(jnp.where(plan[None, :] == experts[:, None], ids[None, :], 0), axis=1)
    here = jnp.sum(jnp.where(ids[None, :] == experts[:, None], plan[None, :], 0), axis=1)
    own_code = 2 * jnp.concatenate([experts, spare_host])
    spare_code = 2 * jnp.concatenate([here, experts]) + 1
    is_own = codes[:, None, :] == own_code[None, :, None]
    is_spare = codes[:, None, :] == spare_code[None, :, None]
    landed = is_own | is_spare
    at = jnp.arange(rows, dtype=jnp.int32)
    before = (at[:, None] < at[None, :]).astype(BF)
    position = dot(landed.astype(BF), before, ((2,), (0,)))
    fits = position < CAP
    kept = (is_own[:, :count] & fits[:, :count]) | (is_spare[:, count:] & fits[:, count:])
    rank = dot(kept.astype(BF), before, ((2,), (0,)))
    slot = jnp.arange(2 * CAP, dtype=F32)
    hit = kept[:, :, None, :] & (rank[:, :, None, :] == slot[None, None, :, None])
    token = at // TOPK + 1
    tokens_of = jnp.sum(jnp.where(hit, token[None, None, None, :], 0), axis=3)
    group = jnp.arange(groups, dtype=jnp.int32)[:, None, None]
    tokens_of = jnp.where(tokens_of > 0, tokens_of - 1 + group * (rows // TOPK), -1)
    weight_of = jnp.sum(jnp.where(hit, weights[:, None, None, :], 0.0), axis=3)
    order = lambda v: v.transpose(1, 0, 2).reshape(-1)
    return order(tokens_of), order(weight_of)


def halves(value):
    high = lax.reduce_precision(value, 8, 7)
    return high.astype(BF), (value - high).astype(BF)


def host_codes(plan):
    hosts = plan.shape[0]
    count = hosts // lax.axis_size("zh")
    experts = lax.axis_index("zh") * count + jnp.arange(count, dtype=jnp.int32)
    ids = jnp.arange(hosts, dtype=jnp.int32)
    spare_host = jnp.sum(jnp.where(plan[None, :] == experts[:, None], ids[None, :], 0), axis=1)
    here = jnp.sum(jnp.where(ids[None, :] == experts[:, None], plan[None, :], 0), axis=1)
    own_code = 2 * jnp.concatenate([experts, spare_host])
    spare_code = 2 * jnp.concatenate([here, experts]) + 1
    return jnp.stack([own_code, spare_code], axis=1).astype(F32)


def ahead(shape, axis):
    return lax.broadcasted_iota(jnp.int32, shape, axis)


def one(mask, dtype=F32):
    return jnp.where(mask, 1.0, 0.0).astype(dtype)


def route_kernel(index, group, came, codes, rows_out, high_out, mid_out):
    count, rows = codes.shape[0] // 2, group * TOPK
    feats, lines = came.shape[2], 2 * group
    before = one(ahead((rows, rows), 0) < ahead((rows, rows), 1), BF)
    own_code, spare_code = codes[:, 0:1], codes[:, 1:2]
    table = jnp.zeros((4 * count, 2 * group), F32)
    for g in range(2):
        info = came[g, lines : lines + 16, index * rows : (index + 1) * rows].astype(F32)
        code, high, mid = info[0:1], info[1:2], info[2:3]
        own, spare = one(code == own_code), one(code == spare_code)
        position = dot((own + spare).astype(BF), before, ((1,), (0,)))
        fits = position < CAP
        own, spare = jnp.where(fits, own, 0.0), jnp.where(fits, spare, 0.0)
        kept = own[:count] + spare[count:]
        rank = dot(kept.astype(BF), before, ((1,), (0,)))
        facts = jnp.concatenate([kept, kept * rank, kept * high, kept * mid], axis=0).astype(BF)
        shape = (rows, 2 * group)
        to_token = one(ahead(shape, 0) // TOPK + g * group == ahead(shape, 1), BF)
        table = table + dot(facts, to_token, ((1,), (0,)))
    table = table.astype(BF)
    slots = count * 4 * CAP
    shape = (slots, count)
    spread = one(ahead(shape, 0) // (4 * CAP) == ahead(shape, 1), BF)
    kept, rank, high, mid = (
        dot(spread, table[i * count : (i + 1) * count], ((1,), (0,))) for i in range(4)
    )
    shape = (slots, 2 * group)
    slot, token = ahead(shape, 0), ahead(shape, 1)
    turn = (slot % (2 * CAP)).astype(F32)
    hot = (kept > 0.5) & (rank == turn) & ((slot // (2 * CAP)) % 2 == token // group)
    high_out[...] = jnp.where(hot, high, 0.0).astype(BF)
    mid_out[...] = jnp.where(hot, mid, 0.0).astype(BF)
    hot = one(hot, BF)
    for p in range(2):
        both = jnp.concatenate([came[2 * p + g, index * group : (index + 1) * group] for g in range(2)], axis=0)
        rows_out[:, p * feats : (p + 1) * feats] = dot(hot, both, ((1,), (0,))).astype(BF)


def route(came, codes, index, group):
    slots, feats = codes.shape[0] // 2 * 4 * CAP, came.shape[2]
    vmem = pl.BlockSpec(memory_space=pltpu.VMEM)
    shape = lambda width: jax.ShapeDtypeStruct((slots, width), BF)
    return pl.pallas_call(
        functools.partial(route_kernel, index, group),
        out_shape=[shape(2 * feats), shape(2 * group), shape(2 * group)],
        in_specs=[vmem, vmem],
        out_specs=[vmem, vmem, vmem],
        compiler_params=pltpu.CompilerParams(vmem_limit_bytes=32 << 20),
        cost_estimate=pl.CostEstimate(flops=2 * slots * 2 * group * 2 * feats, bytes_accessed=2 << 20, transcendentals=0),
    )(came, codes)


def local(tokens, w_gate, w_down, expert_ids, route_weight, replica_pick, old_plan, new_plan):
    batches, group, feats = tokens.shape
    peers = lax.axis_size("y") * lax.axis_size("x")
    code = (2 * expert_ids + (replica_pick & 1)).astype(BF)
    info = jnp.stack([code, *halves(route_weight)]).reshape(3, feats)
    sent = jnp.concatenate([tokens.reshape(-1, feats), jnp.pad(info, ((0, 13), (0, 0)))])
    sent = jnp.broadcast_to(sent[None], (4, *sent.shape))
    came = lax.all_to_all(sent, ("p", "zh"), 0, 0, tiled=True)
    plans = [host_codes(old_plan), host_codes(new_plan)]

    gate_parts, down_parts = cut_weights(w_gate, w_down)
    gate_far = swap(gate_parts[2], "m")

    outs, scales = [], []
    for index in range(batches):
        rows, high, mid = route(came, plans[index], index, group)
        scales.append((high, mid))
        rows = rows.reshape(peers, -1, rows.shape[1])
        if index == 0:
            rows, gate_far, down_ready = lax.optimization_barrier((rows, gate_far, down_parts[2]))
            down_far = swap(down_ready, "m")
            gate_own = order(gate_parts[0], gate_far[0])
            gate_other = swap(order(gate_parts[1], gate_far[1]), "k")
            down_own = order(down_parts[0], down_far[0])
            down_other = swap(order(down_parts[1], down_far[1]), "k")
        else:
            rows, gate_other, down_other = lax.optimization_barrier((rows, gate_other, down_other))
        rows = lax.all_to_all(rows, ("y", "x"), 0, 0, tiled=True).reshape(-1, rows.shape[2])
        if outs:
            rows, _ = lax.optimization_barrier((rows, outs[0]))

        send = dot(rows, gate_other, ((1,), (1,)), BF)
        part = dot(rows, gate_own, ((1,), (1,)))
        part = part + swap(send, "k").astype(F32)
        gate = part + swap(part.astype(BF), "m").astype(F32)
        hidden = jax.nn.silu(gate).astype(BF)
        hidden_other = swap(hidden, "k")
        out = dot(hidden, down_own, ((1,), (0,))) + dot(hidden_other, down_other, ((1,), (0,)))
        outs.append(out.astype(BF).reshape(peers, -1, out.shape[1]))

    outputs = []
    for out, (high, mid) in zip(outs, scales):
        back = lax.all_to_all(out, ("y", "x"), 0, 0, tiled=True).reshape(-1, out.shape[2])
        mixed = dot(high, back, ((0,), (0,))) + dot(mid, back, ((0,), (0,)))
        outputs.append(mixed.astype(BF).reshape(2, group, 2, feats))
    mixed = jnp.stack(outputs).transpose(3, 1, 0, 2, 4).reshape(4, batches * group, feats)
    terms = lax.all_to_all(mixed, ("p", "zh"), 0, 0, tiled=True)
    return jnp.sum(terms.astype(F32), axis=0).astype(BF).reshape(batches, group, feats)


def solution(mesh):
    names = tuple(name for name, _ in SPLIT)
    cut = Mesh(mesh.devices.reshape([size for _, size in SPLIT]), names)
    dp, expert = ("p", "m", "k"), ("zh", "y", "x")
    placed = (
        P(None, expert, dp),
        P(expert, dp, None),
        P(expert, dp, None),
        P(None, expert, None),
        P(None, expert, None),
        P(None, expert, None),
        P(),
        P(),
    )
    return jax.shard_map(
        local, mesh=cut, in_specs=placed, out_specs=P(None, expert, dp), check_vma=False
    )
```

```python
import functools

import jax
import jax.numpy as jnp
from jax import lax
from jax.experimental import pallas as pl
from jax.experimental.pallas import tpu as pltpu
from jax.sharding import Mesh
from jax.sharding import PartitionSpec as P

TOPK = 8
CAP = 4
BF = jnp.bfloat16
F32 = jnp.float32

SPLIT = (("p", 2), ("m", 2), ("k", 2), ("zh", 2), ("y", 8), ("x", 4))


def dot(a, b, dims, out=F32):
    return lax.dot_general(a, b, (dims, ((), ())), preferred_element_type=out)


def swap(array, *axes):
    last = 2 ** len(axes) - 1
    return lax.ppermute(array, axes, [(i, last - i) for i in range(last + 1)])


def cut_kernel(place, gate, down, *outs):
    m, k = place[0], place[1]
    width = gate.shape[2] // 8
    for which, weight in enumerate((gate, down)):
        mine, for_k, for_m = outs[3 * which : 3 * which + 3]
        for dm, dk, out in ((0, 0, mine), (0, 1, for_k), (1, 0, for_m.at[0]), (1, 1, for_m.at[1])):
            for p in range(2):
                at = (4 * p + 2 * (m ^ dm) + (k ^ dk)) * width
                out[:, p * width : (p + 1) * width] = weight[0, :, pl.ds(pl.multiple_of(at, width), width)]


def cut_weights(gate, down):
    _, hidden, feats = gate.shape
    place = jnp.stack([lax.axis_index("m"), lax.axis_index("k")]).astype(jnp.int32)
    rows = hidden // 2
    whole = pl.BlockSpec((1, rows, feats), lambda i: (0, i, 0))
    one = pl.BlockSpec((rows, feats // 4), lambda i: (i, 0))
    two = pl.BlockSpec((2, rows, feats // 4), lambda i: (0, i, 0))
    shape = lambda *lead: jax.ShapeDtypeStruct((*lead, hidden, feats // 4), BF)
    parts = pl.pallas_call(
        cut_kernel,
        out_shape=[shape(), shape(), shape(2)] * 2,
        grid=(2,),
        in_specs=[pl.BlockSpec(memory_space=pltpu.SMEM), whole, whole],
        out_specs=[one, one, two] * 2,
        compiler_params=pltpu.CompilerParams(vmem_limit_bytes=32 << 20),
        cost_estimate=pl.CostEstimate(flops=0, bytes_accessed=4 * gate.size * 2, transcendentals=0),
    )(place, gate, down)
    return parts[:3], parts[3:]


def order(near, far):
    m = lax.axis_index("m")
    first = jnp.where(m == 0, near, far)
    second = jnp.where(m == 0, far, near)
    return jnp.concatenate([first, second], axis=0)


def slots(codes, weights, plan):
    groups, rows = codes.shape
    hosts = plan.shape[0]
    count = hosts // lax.axis_size("zh")
    experts = lax.axis_index("zh") * count + jnp.arange(count, dtype=jnp.int32)
    ids = jnp.arange(hosts, dtype=jnp.int32)
    spare_host = jnp.sum(jnp.where(plan[None, :] == experts[:, None], ids[None, :], 0), axis=1)
    here = jnp.sum(jnp.where(ids[None, :] == experts[:, None], plan[None, :], 0), axis=1)
    own_code = 2 * jnp.concatenate([experts, spare_host])
    spare_code = 2 * jnp.concatenate([here, experts]) + 1
    is_own = codes[:, None, :] == own_code[None, :, None]
    is_spare = codes[:, None, :] == spare_code[None, :, None]
    landed = is_own | is_spare
    at = jnp.arange(rows, dtype=jnp.int32)
    before = (at[:, None] < at[None, :]).astype(BF)
    position = dot(landed.astype(BF), before, ((2,), (0,)))
    fits = position < CAP
    kept = (is_own[:, :count] & fits[:, :count]) | (is_spare[:, count:] & fits[:, count:])
    rank = dot(kept.astype(BF), before, ((2,), (0,)))
    slot = jnp.arange(2 * CAP, dtype=F32)
    hit = kept[:, :, None, :] & (rank[:, :, None, :] == slot[None, None, :, None])
    token = at // TOPK + 1
    tokens_of = jnp.sum(jnp.where(hit, token[None, None, None, :], 0), axis=3)
    group = jnp.arange(groups, dtype=jnp.int32)[:, None, None]
    tokens_of = jnp.where(tokens_of > 0, tokens_of - 1 + group * (rows // TOPK), -1)
    weight_of = jnp.sum(jnp.where(hit, weights[:, None, None, :], 0.0), axis=3)
    order = lambda v: v.transpose(1, 0, 2).reshape(-1)
    return order(tokens_of), order(weight_of)


def halves(value):
    high = lax.reduce_precision(value, 8, 7)
    return high.astype(BF), (value - high).astype(BF)


def host_codes(plan):
    hosts = plan.shape[0]
    count = hosts // lax.axis_size("zh")
    experts = lax.axis_index("zh") * count + jnp.arange(count, dtype=jnp.int32)
    ids = jnp.arange(hosts, dtype=jnp.int32)
    spare_host = jnp.sum(jnp.where(plan[None, :] == experts[:, None], ids[None, :], 0), axis=1)
    here = jnp.sum(jnp.where(ids[None, :] == experts[:, None], plan[None, :], 0), axis=1)
    own_code = 2 * jnp.concatenate([experts, spare_host])
    spare_code = 2 * jnp.concatenate([here, experts]) + 1
    return jnp.stack([own_code, spare_code], axis=1).astype(F32)


def ahead(shape, axis):
    return lax.broadcasted_iota(jnp.int32, shape, axis)


def one(mask, dtype=F32):
    return jnp.where(mask, 1.0, 0.0).astype(dtype)


def route_kernel(index, group, came, codes, rows_out, high_out, mid_out):
    count, rows = codes.shape[0] // 2, group * TOPK
    feats, lines = came.shape[2], 2 * group
    before = one(ahead((rows, rows), 0) < ahead((rows, rows), 1), BF)
    own_code, spare_code = codes[:, 0:1], codes[:, 1:2]
    table = jnp.zeros((4 * count, 2 * group), F32)
    for g in range(2):
        info = came[g, lines : lines + 16, index * rows : (index + 1) * rows].astype(F32)
        code, high, mid = info[0:1], info[1:2], info[2:3]
        own, spare = one(code == own_code), one(code == spare_code)
        position = dot((own + spare).astype(BF), before, ((1,), (0,)))
        fits = position < CAP
        own, spare = jnp.where(fits, own, 0.0), jnp.where(fits, spare, 0.0)
        kept = own[:count] + spare[count:]
        rank = dot(kept.astype(BF), before, ((1,), (0,)))
        facts = jnp.concatenate([kept, kept * rank, kept * high, kept * mid], axis=0).astype(BF)
        shape = (rows, 2 * group)
        to_token = one(ahead(shape, 0) // TOPK + g * group == ahead(shape, 1), BF)
        table = table + dot(facts, to_token, ((1,), (0,)))
    table = table.astype(BF)
    slots = count * 4 * CAP
    shape = (slots, count)
    spread = one(ahead(shape, 0) // (4 * CAP) == ahead(shape, 1), BF)
    kept, rank, high, mid = (
        dot(spread, table[i * count : (i + 1) * count], ((1,), (0,))) for i in range(4)
    )
    shape = (slots, 2 * group)
    slot, token = ahead(shape, 0), ahead(shape, 1)
    turn = (slot % (2 * CAP)).astype(F32)
    hot = (kept > 0.5) & (rank == turn) & ((slot // (2 * CAP)) % 2 == token // group)
    high_out[...] = jnp.where(hot, high, 0.0).astype(BF)
    mid_out[...] = jnp.where(hot, mid, 0.0).astype(BF)
    hot = one(hot, BF)
    for p in range(2):
        both = jnp.concatenate([came[2 * p + g, index * group : (index + 1) * group] for g in range(2)], axis=0)
        rows_out[:, p * feats : (p + 1) * feats] = dot(hot, both, ((1,), (0,))).astype(BF)


def route(came, codes, index, group):
    slots, feats = codes.shape[0] // 2 * 4 * CAP, came.shape[2]
    vmem = pl.BlockSpec(memory_space=pltpu.VMEM)
    shape = lambda width: jax.ShapeDtypeStruct((slots, width), BF)
    return pl.pallas_call(
        functools.partial(route_kernel, index, group),
        out_shape=[shape(2 * feats), shape(2 * group), shape(2 * group)],
        in_specs=[vmem, vmem],
        out_specs=[vmem, vmem, vmem],
        compiler_params=pltpu.CompilerParams(vmem_limit_bytes=32 << 20),
        cost_estimate=pl.CostEstimate(flops=2 * slots * 2 * group * 2 * feats, bytes_accessed=2 << 20, transcendentals=0),
    )(came, codes)


def local(tokens, w_gate, w_down, expert_ids, route_weight, replica_pick, old_plan, new_plan):
    batches, group, feats = tokens.shape
    peers = lax.axis_size("y") * lax.axis_size("x")
    code = (2 * expert_ids + (replica_pick & 1)).astype(BF)
    info = jnp.stack([code, *halves(route_weight)]).reshape(3, feats)
    sent = jnp.concatenate([tokens.reshape(-1, feats), jnp.pad(info, ((0, 13), (0, 0)))])
    sent = jnp.broadcast_to(sent[None], (4, *sent.shape))
    came = lax.all_to_all(sent, ("p", "zh"), 0, 0, tiled=True)
    plans = [host_codes(old_plan), host_codes(new_plan)]

    gate_parts, down_parts = cut_weights(w_gate, w_down)
    came, gate_sent = lax.optimization_barrier((came, gate_parts[2]))
    gate_far = swap(gate_sent, "m")
    gate_own = order(gate_parts[0], gate_far[0])
    gate_other = swap(order(gate_parts[1], gate_far[1]), "k")
    _, down_sent = lax.optimization_barrier((gate_far, down_parts[2]))
    down_far = swap(down_sent, "m")
    down_own = order(down_parts[0], down_far[0])
    down_other = swap(order(down_parts[1], down_far[1]), "k")

    outs, scales = [], []
    for index in range(batches):
        rows, high, mid = route(came, plans[index], index, group)
        scales.append((high, mid))
        rows = rows.reshape(peers, -1, rows.shape[1])
        if outs:
            rows, gate_other = lax.optimization_barrier((rows, gate_other))
        rows = lax.all_to_all(rows, ("y", "x"), 0, 0, tiled=True).reshape(-1, rows.shape[2])
        if outs:
            rows, _ = lax.optimization_barrier((rows, outs[0]))

        send = dot(rows, gate_other, ((1,), (1,)), BF)
        part = dot(rows, gate_own, ((1,), (1,)))
        part = part + swap(send, "k").astype(F32)
        gate = part + swap(part.astype(BF), "m").astype(F32)
        hidden = jax.nn.silu(gate).astype(BF)
        hidden_other = swap(hidden, "k")
        out = dot(hidden, down_own, ((1,), (0,))) + dot(hidden_other, down_other, ((1,), (0,)))
        outs.append(out.astype(BF).reshape(peers, -1, out.shape[1]))

    outputs = []
    for out, (high, mid) in zip(outs, scales):
        back = lax.all_to_all(out, ("y", "x"), 0, 0, tiled=True).reshape(-1, out.shape[2])
        mixed = dot(high, back, ((0,), (0,))) + dot(mid, back, ((0,), (0,)))
        outputs.append(mixed.astype(BF).reshape(2, group, 2, feats))
    mixed = jnp.stack(outputs).transpose(3, 1, 0, 2, 4).reshape(4, batches * group, feats)
    terms = lax.all_to_all(mixed, ("p", "zh"), 0, 0, tiled=True)
    return jnp.sum(terms.astype(F32), axis=0).astype(BF).reshape(batches, group, feats)


def solution(mesh):
    names = tuple(name for name, _ in SPLIT)
    cut = Mesh(mesh.devices.reshape([size for _, size in SPLIT]), names)
    dp, expert = ("p", "m", "k"), ("zh", "y", "x")
    placed = (
        P(None, expert, dp),
        P(expert, dp, None),
        P(expert, dp, None),
        P(None, expert, None),
        P(None, expert, None),
        P(None, expert, None),
        P(),
        P(),
    )
    return jax.shard_map(
        local, mesh=cut, in_specs=placed, out_specs=P(None, expert, dp), check_vma=False
    )
```

```python
import functools

import jax
import jax.numpy as jnp
from jax import lax
from jax.experimental import pallas as pl
from jax.experimental.pallas import tpu as pltpu
from jax.sharding import Mesh
from jax.sharding import PartitionSpec as P

TOPK = 8
CAP = 4
BF = jnp.bfloat16
F32 = jnp.float32

SPLIT = (("p", 2), ("m", 2), ("k", 2), ("zh", 2), ("y", 8), ("x", 4))


def dot(a, b, dims, out=F32):
    return lax.dot_general(a, b, (dims, ((), ())), preferred_element_type=out)


def swap(array, *axes):
    last = 2 ** len(axes) - 1
    return lax.ppermute(array, axes, [(i, last - i) for i in range(last + 1)])


def cut_kernel(place, gate, down, *outs):
    m, k = place[0], place[1]
    width = gate.shape[2] // 8
    for which, weight in enumerate((gate, down)):
        mine, for_k, for_m = outs[3 * which : 3 * which + 3]
        for dm, dk, out in ((0, 0, mine), (0, 1, for_k), (1, 0, for_m.at[0]), (1, 1, for_m.at[1])):
            for p in range(2):
                at = (4 * p + 2 * (m ^ dm) + (k ^ dk)) * width
                out[:, p * width : (p + 1) * width] = weight[0, :, pl.ds(pl.multiple_of(at, width), width)]


def cut_weights(gate, down):
    _, hidden, feats = gate.shape
    place = jnp.stack([lax.axis_index("m"), lax.axis_index("k")]).astype(jnp.int32)
    rows = hidden // 2
    whole = pl.BlockSpec((1, rows, feats), lambda i: (0, i, 0))
    one = pl.BlockSpec((rows, feats // 4), lambda i: (i, 0))
    two = pl.BlockSpec((2, rows, feats // 4), lambda i: (0, i, 0))
    shape = lambda *lead: jax.ShapeDtypeStruct((*lead, hidden, feats // 4), BF)
    parts = pl.pallas_call(
        cut_kernel,
        out_shape=[shape(), shape(), shape(2)] * 2,
        grid=(2,),
        in_specs=[pl.BlockSpec(memory_space=pltpu.SMEM), whole, whole],
        out_specs=[one, one, two] * 2,
        compiler_params=pltpu.CompilerParams(vmem_limit_bytes=32 << 20),
        cost_estimate=pl.CostEstimate(flops=0, bytes_accessed=4 * gate.size * 2, transcendentals=0),
    )(place, gate, down)
    return parts[:3], parts[3:]


def order(near, far):
    m = lax.axis_index("m")
    first = jnp.where(m == 0, near, far)
    second = jnp.where(m == 0, far, near)
    return jnp.concatenate([first, second], axis=0)


def slots(codes, weights, plan):
    groups, rows = codes.shape
    hosts = plan.shape[0]
    count = hosts // lax.axis_size("zh")
    experts = lax.axis_index("zh") * count + jnp.arange(count, dtype=jnp.int32)
    ids = jnp.arange(hosts, dtype=jnp.int32)
    spare_host = jnp.sum(jnp.where(plan[None, :] == experts[:, None], ids[None, :], 0), axis=1)
    here = jnp.sum(jnp.where(ids[None, :] == experts[:, None], plan[None, :], 0), axis=1)
    own_code = 2 * jnp.concatenate([experts, spare_host])
    spare_code = 2 * jnp.concatenate([here, experts]) + 1
    is_own = codes[:, None, :] == own_code[None, :, None]
    is_spare = codes[:, None, :] == spare_code[None, :, None]
    landed = is_own | is_spare
    at = jnp.arange(rows, dtype=jnp.int32)
    before = (at[:, None] < at[None, :]).astype(BF)
    position = dot(landed.astype(BF), before, ((2,), (0,)))
    fits = position < CAP
    kept = (is_own[:, :count] & fits[:, :count]) | (is_spare[:, count:] & fits[:, count:])
    rank = dot(kept.astype(BF), before, ((2,), (0,)))
    slot = jnp.arange(2 * CAP, dtype=F32)
    hit = kept[:, :, None, :] & (rank[:, :, None, :] == slot[None, None, :, None])
    token = at // TOPK + 1
    tokens_of = jnp.sum(jnp.where(hit, token[None, None, None, :], 0), axis=3)
    group = jnp.arange(groups, dtype=jnp.int32)[:, None, None]
    tokens_of = jnp.where(tokens_of > 0, tokens_of - 1 + group * (rows // TOPK), -1)
    weight_of = jnp.sum(jnp.where(hit, weights[:, None, None, :], 0.0), axis=3)
    order = lambda v: v.transpose(1, 0, 2).reshape(-1)
    return order(tokens_of), order(weight_of)


def halves(value):
    high = lax.reduce_precision(value, 8, 7)
    return high.astype(BF), (value - high).astype(BF)


def host_codes(plan):
    hosts = plan.shape[0]
    count = hosts // lax.axis_size("zh")
    experts = lax.axis_index("zh") * count + jnp.arange(count, dtype=jnp.int32)
    ids = jnp.arange(hosts, dtype=jnp.int32)
    spare_host = jnp.sum(jnp.where(plan[None, :] == experts[:, None], ids[None, :], 0), axis=1)
    here = jnp.sum(jnp.where(ids[None, :] == experts[:, None], plan[None, :], 0), axis=1)
    own_code = 2 * jnp.concatenate([experts, spare_host])
    spare_code = 2 * jnp.concatenate([here, experts]) + 1
    return jnp.stack([own_code, spare_code], axis=1).astype(F32)


def ahead(shape, axis):
    return lax.broadcasted_iota(jnp.int32, shape, axis)


def one(mask, dtype=F32):
    return jnp.where(mask, 1.0, 0.0).astype(dtype)


def route_kernel(index, group, came, codes, rows_out, high_out, mid_out):
    count, rows = codes.shape[0] // 2, group * TOPK
    feats, lines = came.shape[2], 2 * group
    before = one(ahead((rows, rows), 0) < ahead((rows, rows), 1), BF)
    own_code, spare_code = codes[:, 0:1], codes[:, 1:2]
    table = jnp.zeros((4 * count, 2 * group), F32)
    for g in range(2):
        info = came[g, lines : lines + 16, index * rows : (index + 1) * rows].astype(F32)
        code, high, mid = info[0:1], info[1:2], info[2:3]
        own, spare = one(code == own_code), one(code == spare_code)
        position = dot((own + spare).astype(BF), before, ((1,), (0,)))
        fits = position < CAP
        own, spare = jnp.where(fits, own, 0.0), jnp.where(fits, spare, 0.0)
        kept = own[:count] + spare[count:]
        rank = dot(kept.astype(BF), before, ((1,), (0,)))
        facts = jnp.concatenate([kept, kept * rank, kept * high, kept * mid], axis=0).astype(BF)
        shape = (rows, 2 * group)
        to_token = one(ahead(shape, 0) // TOPK + g * group == ahead(shape, 1), BF)
        table = table + dot(facts, to_token, ((1,), (0,)))
    table = table.astype(BF)
    slots = count * 4 * CAP
    shape = (slots, count)
    spread = one(ahead(shape, 0) // (4 * CAP) == ahead(shape, 1), BF)
    kept, rank, high, mid = (
        dot(spread, table[i * count : (i + 1) * count], ((1,), (0,))) for i in range(4)
    )
    shape = (slots, 2 * group)
    slot, token = ahead(shape, 0), ahead(shape, 1)
    turn = (slot % (2 * CAP)).astype(F32)
    hot = (kept > 0.5) & (rank == turn) & ((slot // (2 * CAP)) % 2 == token // group)
    high_out[...] = jnp.where(hot, high, 0.0).astype(BF)
    mid_out[...] = jnp.where(hot, mid, 0.0).astype(BF)
    hot = one(hot, BF)
    for p in range(2):
        both = jnp.concatenate([came[2 * p + g, index * group : (index + 1) * group] for g in range(2)], axis=0)
        rows_out[:, p * feats : (p + 1) * feats] = dot(hot, both, ((1,), (0,))).astype(BF)


def route(came, codes, index, group):
    slots, feats = codes.shape[0] // 2 * 4 * CAP, came.shape[2]
    vmem = pl.BlockSpec(memory_space=pltpu.VMEM)
    shape = lambda width: jax.ShapeDtypeStruct((slots, width), BF)
    return pl.pallas_call(
        functools.partial(route_kernel, index, group),
        out_shape=[shape(2 * feats), shape(2 * group), shape(2 * group)],
        in_specs=[vmem, vmem],
        out_specs=[vmem, vmem, vmem],
        compiler_params=pltpu.CompilerParams(vmem_limit_bytes=32 << 20),
        cost_estimate=pl.CostEstimate(flops=2 * slots * 2 * group * 2 * feats, bytes_accessed=2 << 20, transcendentals=0),
    )(came, codes)


def local(tokens, w_gate, w_down, expert_ids, route_weight, replica_pick, old_plan, new_plan):
    batches, group, feats = tokens.shape
    peers = lax.axis_size("y") * lax.axis_size("x")
    code = (2 * expert_ids + (replica_pick & 1)).astype(BF)
    info = jnp.stack([code, *halves(route_weight)]).reshape(3, feats)
    sent = jnp.concatenate([tokens.reshape(-1, feats), jnp.pad(info, ((0, 13), (0, 0)))])
    sent = jnp.broadcast_to(sent[None], (4, *sent.shape))
    came = lax.all_to_all(sent, ("p", "zh"), 0, 0, tiled=True)
    plans = [host_codes(old_plan), host_codes(new_plan)]

    gate_parts, down_parts = cut_weights(w_gate, w_down)
    came, gate_sent = lax.optimization_barrier((came, gate_parts[2]))
    gate_far = swap(gate_sent, "m")
    routed = [route(came, plans[index], index, group) for index in range(batches)]
    gate_far, routed[1] = lax.optimization_barrier((gate_far, routed[1]))
    gate_own = order(gate_parts[0], gate_far[0])
    gate_other = swap(order(gate_parts[1], gate_far[1]), "k")
    _, down_sent = lax.optimization_barrier((gate_far, down_parts[2]))
    down_far = swap(down_sent, "m")
    down_own = order(down_parts[0], down_far[0])
    down_other = swap(order(down_parts[1], down_far[1]), "k")

    outs, scales = [], []
    for index in range(batches):
        rows, high, mid = routed[index]
        scales.append((high, mid))
        rows = rows.reshape(peers, -1, rows.shape[1])
        rows = lax.all_to_all(rows, ("y", "x"), 0, 0, tiled=True).reshape(-1, rows.shape[2])
        if outs:
            rows, _ = lax.optimization_barrier((rows, outs[0]))

        send = dot(rows, gate_other, ((1,), (1,)), BF)
        part = lax.optimization_barrier(dot(rows, gate_own, ((1,), (1,))))
        part = part + swap(send, "k").astype(F32)
        gate = part + swap(part.astype(BF), "m").astype(F32)
        hidden = jax.nn.silu(gate).astype(BF)
        hidden_other = swap(hidden, "k")
        out = dot(hidden, down_own, ((1,), (0,))) + dot(hidden_other, down_other, ((1,), (0,)))
        outs.append(out.astype(BF).reshape(peers, -1, out.shape[1]))

    outputs = []
    for out, (high, mid) in zip(outs, scales):
        back = lax.all_to_all(out, ("y", "x"), 0, 0, tiled=True).reshape(-1, out.shape[2])
        mixed = dot(high, back, ((0,), (0,))) + dot(mid, back, ((0,), (0,)))
        outputs.append(mixed.astype(BF).reshape(2, group, 2, feats))
    mixed = jnp.stack(outputs).transpose(3, 1, 0, 2, 4).reshape(4, batches * group, feats)
    terms = lax.all_to_all(mixed, ("p", "zh"), 0, 0, tiled=True)
    return jnp.sum(terms.astype(F32), axis=0).astype(BF).reshape(batches, group, feats)


def solution(mesh):
    names = tuple(name for name, _ in SPLIT)
    cut = Mesh(mesh.devices.reshape([size for _, size in SPLIT]), names)
    dp, expert = ("p", "m", "k"), ("zh", "y", "x")
    placed = (
        P(None, expert, dp),
        P(expert, dp, None),
        P(expert, dp, None),
        P(None, expert, None),
        P(None, expert, None),
        P(None, expert, None),
        P(),
        P(),
    )
    return jax.shard_map(
        local, mesh=cut, in_specs=placed, out_specs=P(None, expert, dp), check_vma=False
    )
```

```python
import functools

import jax
import jax.numpy as jnp
from jax import lax
from jax.experimental import pallas as pl
from jax.experimental.pallas import tpu as pltpu
from jax.sharding import Mesh
from jax.sharding import PartitionSpec as P

TOPK = 8
CAP = 4
BF = jnp.bfloat16
F32 = jnp.float32

SPLIT = (("p", 2), ("m", 2), ("k", 2), ("zh", 2), ("y", 8), ("x", 4))


def dot(a, b, dims, out=F32):
    return lax.dot_general(a, b, (dims, ((), ())), preferred_element_type=out)


def swap(array, *axes):
    last = 2 ** len(axes) - 1
    return lax.ppermute(array, axes, [(i, last - i) for i in range(last + 1)])


def cut_kernel(place, gate, down, *outs):
    m, k = place[0], place[1]
    width = gate.shape[2] // 8
    for which, weight in enumerate((gate, down)):
        mine, for_k, for_m = outs[3 * which : 3 * which + 3]
        for dm, dk, out in ((0, 0, mine), (0, 1, for_k), (1, 0, for_m.at[0]), (1, 1, for_m.at[1])):
            for p in range(2):
                at = (4 * p + 2 * (m ^ dm) + (k ^ dk)) * width
                out[:, p * width : (p + 1) * width] = weight[0, :, pl.ds(pl.multiple_of(at, width), width)]


def cut_weights(gate, down):
    _, hidden, feats = gate.shape
    place = jnp.stack([lax.axis_index("m"), lax.axis_index("k")]).astype(jnp.int32)
    rows = hidden // 2
    whole = pl.BlockSpec((1, rows, feats), lambda i: (0, i, 0))
    one = pl.BlockSpec((rows, feats // 4), lambda i: (i, 0))
    two = pl.BlockSpec((2, rows, feats // 4), lambda i: (0, i, 0))
    shape = lambda *lead: jax.ShapeDtypeStruct((*lead, hidden, feats // 4), BF)
    parts = pl.pallas_call(
        cut_kernel,
        out_shape=[shape(), shape(), shape(2)] * 2,
        grid=(2,),
        in_specs=[pl.BlockSpec(memory_space=pltpu.SMEM), whole, whole],
        out_specs=[one, one, two] * 2,
        compiler_params=pltpu.CompilerParams(vmem_limit_bytes=32 << 20),
        cost_estimate=pl.CostEstimate(flops=0, bytes_accessed=4 * gate.size * 2, transcendentals=0),
    )(place, gate, down)
    return parts[:3], parts[3:]


def order(near, far):
    m = lax.axis_index("m")
    first = jnp.where(m == 0, near, far)
    second = jnp.where(m == 0, far, near)
    return jnp.concatenate([first, second], axis=0)


def slots(codes, weights, plan):
    groups, rows = codes.shape
    hosts = plan.shape[0]
    count = hosts // lax.axis_size("zh")
    experts = lax.axis_index("zh") * count + jnp.arange(count, dtype=jnp.int32)
    ids = jnp.arange(hosts, dtype=jnp.int32)
    spare_host = jnp.sum(jnp.where(plan[None, :] == experts[:, None], ids[None, :], 0), axis=1)
    here = jnp.sum(jnp.where(ids[None, :] == experts[:, None], plan[None, :], 0), axis=1)
    own_code = 2 * jnp.concatenate([experts, spare_host])
    spare_code = 2 * jnp.concatenate([here, experts]) + 1
    is_own = codes[:, None, :] == own_code[None, :, None]
    is_spare = codes[:, None, :] == spare_code[None, :, None]
    landed = is_own | is_spare
    at = jnp.arange(rows, dtype=jnp.int32)
    before = (at[:, None] < at[None, :]).astype(BF)
    position = dot(landed.astype(BF), before, ((2,), (0,)))
    fits = position < CAP
    kept = (is_own[:, :count] & fits[:, :count]) | (is_spare[:, count:] & fits[:, count:])
    rank = dot(kept.astype(BF), before, ((2,), (0,)))
    slot = jnp.arange(2 * CAP, dtype=F32)
    hit = kept[:, :, None, :] & (rank[:, :, None, :] == slot[None, None, :, None])
    token = at // TOPK + 1
    tokens_of = jnp.sum(jnp.where(hit, token[None, None, None, :], 0), axis=3)
    group = jnp.arange(groups, dtype=jnp.int32)[:, None, None]
    tokens_of = jnp.where(tokens_of > 0, tokens_of - 1 + group * (rows // TOPK), -1)
    weight_of = jnp.sum(jnp.where(hit, weights[:, None, None, :], 0.0), axis=3)
    order = lambda v: v.transpose(1, 0, 2).reshape(-1)
    return order(tokens_of), order(weight_of)


def halves(value):
    high = lax.reduce_precision(value, 8, 7)
    return high.astype(BF), (value - high).astype(BF)


def host_codes(plan):
    hosts = plan.shape[0]
    count = hosts // lax.axis_size("zh")
    experts = lax.axis_index("zh") * count + jnp.arange(count, dtype=jnp.int32)
    ids = jnp.arange(hosts, dtype=jnp.int32)
    spare_host = jnp.sum(jnp.where(plan[None, :] == experts[:, None], ids[None, :], 0), axis=1)
    here = jnp.sum(jnp.where(ids[None, :] == experts[:, None], plan[None, :], 0), axis=1)
    own_code = 2 * jnp.concatenate([experts, spare_host])
    spare_code = 2 * jnp.concatenate([here, experts]) + 1
    return jnp.stack([own_code, spare_code], axis=1).astype(F32)


def ahead(shape, axis):
    return lax.broadcasted_iota(jnp.int32, shape, axis)


def one(mask, dtype=F32):
    return jnp.where(mask, 1.0, 0.0).astype(dtype)


def route_kernel(index, group, came, codes, rows_out, high_out, mid_out):
    count, rows = codes.shape[0] // 2, group * TOPK
    feats, lines = came.shape[2], 2 * group
    before = one(ahead((rows, rows), 0) < ahead((rows, rows), 1), BF)
    own_code, spare_code = codes[:, 0:1], codes[:, 1:2]
    table = jnp.zeros((4 * count, 2 * group), F32)
    for g in range(2):
        info = came[g, lines : lines + 16, index * rows : (index + 1) * rows].astype(F32)
        code, high, mid = info[0:1], info[1:2], info[2:3]
        own, spare = one(code == own_code), one(code == spare_code)
        position = dot((own + spare).astype(BF), before, ((1,), (0,)))
        fits = position < CAP
        own, spare = jnp.where(fits, own, 0.0), jnp.where(fits, spare, 0.0)
        kept = own[:count] + spare[count:]
        rank = dot(kept.astype(BF), before, ((1,), (0,)))
        facts = jnp.concatenate([kept, kept * rank, kept * high, kept * mid], axis=0).astype(BF)
        shape = (rows, 2 * group)
        to_token = one(ahead(shape, 0) // TOPK + g * group == ahead(shape, 1), BF)
        table = table + dot(facts, to_token, ((1,), (0,)))
    table = table.astype(BF)
    slots = count * 4 * CAP
    shape = (slots, count)
    spread = one(ahead(shape, 0) // (4 * CAP) == ahead(shape, 1), BF)
    kept, rank, high, mid = (
        dot(spread, table[i * count : (i + 1) * count], ((1,), (0,))) for i in range(4)
    )
    shape = (slots, 2 * group)
    slot, token = ahead(shape, 0), ahead(shape, 1)
    turn = (slot % (2 * CAP)).astype(F32)
    hot = (kept > 0.5) & (rank == turn) & ((slot // (2 * CAP)) % 2 == token // group)
    high_out[...] = jnp.where(hot, high, 0.0).astype(BF)
    mid_out[...] = jnp.where(hot, mid, 0.0).astype(BF)
    hot = one(hot, BF)
    for p in range(2):
        both = jnp.concatenate([came[2 * p + g, index * group : (index + 1) * group] for g in range(2)], axis=0)
        rows_out[:, p * feats : (p + 1) * feats] = dot(hot, both, ((1,), (0,))).astype(BF)


def route(came, codes, index, group):
    slots, feats = codes.shape[0] // 2 * 4 * CAP, came.shape[2]
    vmem = pl.BlockSpec(memory_space=pltpu.VMEM)
    shape = lambda width: jax.ShapeDtypeStruct((slots, width), BF)
    return pl.pallas_call(
        functools.partial(route_kernel, index, group),
        out_shape=[shape(2 * feats), shape(2 * group), shape(2 * group)],
        in_specs=[vmem, vmem],
        out_specs=[vmem, vmem, vmem],
        compiler_params=pltpu.CompilerParams(vmem_limit_bytes=32 << 20),
        cost_estimate=pl.CostEstimate(flops=2 * slots * 2 * group * 2 * feats, bytes_accessed=2 << 20, transcendentals=0),
    )(came, codes)


def gate_kernel(rows, own, other, send_out, part_out):
    send_out[...] = dot(rows[...], other[...], ((1,), (1,))).astype(BF)
    part_out[...] = dot(rows[...], own[...], ((1,), (1,)))


def down_kernel(hidden, hidden_other, own, other, out):
    total = dot(hidden[...], own[...], ((1,), (0,))) + dot(hidden_other[...], other[...], ((1,), (0,)))
    out[...] = total.astype(BF)


def on_rows(kernel, arrays, weights, widths, types):
    count = arrays[0].shape[0]
    block = count // 4
    by_rows = lambda width: pl.BlockSpec((block, width), lambda i: (i, 0))
    whole = lambda weight: pl.BlockSpec(weight.shape, lambda i: (0, 0))
    moved = sum(a.size for a in (*arrays, *weights)) * 2 + 4 * count * sum(widths)
    return pl.pallas_call(
        kernel,
        out_shape=[jax.ShapeDtypeStruct((count, width), held) for width, held in zip(widths, types)],
        grid=(4,),
        in_specs=[*(by_rows(a.shape[1]) for a in arrays), *(whole(w) for w in weights)],
        out_specs=[by_rows(width) for width in widths],
        compiler_params=pltpu.CompilerParams(vmem_limit_bytes=32 << 20),
        cost_estimate=pl.CostEstimate(
            flops=2 * count * sum(w.size for w in weights), bytes_accessed=moved, transcendentals=0
        ),
    )(*arrays, *weights)


def local(tokens, w_gate, w_down, expert_ids, route_weight, replica_pick, old_plan, new_plan):
    batches, group, feats = tokens.shape
    peers = lax.axis_size("y") * lax.axis_size("x")
    code = (2 * expert_ids + (replica_pick & 1)).astype(BF)
    info = jnp.stack([code, *halves(route_weight)]).reshape(3, feats)
    sent = jnp.concatenate([tokens.reshape(-1, feats), jnp.pad(info, ((0, 13), (0, 0)))])
    sent = jnp.broadcast_to(sent[None], (4, *sent.shape))
    came = lax.all_to_all(sent, ("p", "zh"), 0, 0, tiled=True)
    plans = [host_codes(old_plan), host_codes(new_plan)]

    gate_parts, down_parts = cut_weights(w_gate, w_down)
    came, gate_sent = lax.optimization_barrier((came, gate_parts[2]))
    gate_far = swap(gate_sent, "m")
    routed = [route(came, plans[index], index, group) for index in range(batches)]
    gate_far, routed[1] = lax.optimization_barrier((gate_far, routed[1]))
    gate_own = order(gate_parts[0], gate_far[0])
    gate_other = swap(order(gate_parts[1], gate_far[1]), "k")
    _, down_sent = lax.optimization_barrier((gate_far, down_parts[2]))
    down_far = swap(down_sent, "m")
    down_own = order(down_parts[0], down_far[0])
    down_other = swap(order(down_parts[1], down_far[1]), "k")

    outs, scales = [], []
    for index in range(batches):
        rows, high, mid = routed[index]
        scales.append((high, mid))
        rows = rows.reshape(peers, -1, rows.shape[1])
        rows = lax.all_to_all(rows, ("y", "x"), 0, 0, tiled=True).reshape(-1, rows.shape[2])
        if outs:
            rows, _ = lax.optimization_barrier((rows, outs[0]))

        cut = gate_own.shape[0]
        send, part = on_rows(gate_kernel, [rows], [gate_own, gate_other], [cut, cut], [BF, F32])
        part = part + swap(send, "k").astype(F32)
        gate = part + swap(part.astype(BF), "m").astype(F32)
        hidden = jax.nn.silu(gate).astype(BF)
        hidden_other = swap(hidden, "k")
        (out,) = on_rows(down_kernel, [hidden, hidden_other], [down_own, down_other], [rows.shape[1]], [BF])
        outs.append(out.reshape(peers, -1, out.shape[1]))

    outputs = []
    for out, (high, mid) in zip(outs, scales):
        back = lax.all_to_all(out, ("y", "x"), 0, 0, tiled=True).reshape(-1, out.shape[2])
        mixed = dot(high, back, ((0,), (0,))) + dot(mid, back, ((0,), (0,)))
        outputs.append(mixed.astype(BF).reshape(2, group, 2, feats))
    mixed = jnp.stack(outputs).transpose(3, 1, 0, 2, 4).reshape(4, batches * group, feats)
    terms = lax.all_to_all(mixed, ("p", "zh"), 0, 0, tiled=True)
    return jnp.sum(terms.astype(F32), axis=0).astype(BF).reshape(batches, group, feats)


def solution(mesh):
    names = tuple(name for name, _ in SPLIT)
    cut = Mesh(mesh.devices.reshape([size for _, size in SPLIT]), names)
    dp, expert = ("p", "m", "k"), ("zh", "y", "x")
    placed = (
        P(None, expert, dp),
        P(expert, dp, None),
        P(expert, dp, None),
        P(None, expert, None),
        P(None, expert, None),
        P(None, expert, None),
        P(),
        P(),
    )
    return jax.shard_map(
        local, mesh=cut, in_specs=placed, out_specs=P(None, expert, dp), check_vma=False
    )
```

```python
import functools

import jax
import jax.numpy as jnp
from jax import lax
from jax.experimental import pallas as pl
from jax.experimental.pallas import tpu as pltpu
from jax.sharding import Mesh
from jax.sharding import PartitionSpec as P

TOPK = 8
CAP = 4
BF = jnp.bfloat16
F32 = jnp.float32

SPLIT = (("p", 2), ("m", 2), ("k", 2), ("zh", 2), ("y", 8), ("x", 4))


def dot(a, b, dims, out=F32):
    return lax.dot_general(a, b, (dims, ((), ())), preferred_element_type=out)


def swap(array, *axes):
    last = 2 ** len(axes) - 1
    return lax.ppermute(array, axes, [(i, last - i) for i in range(last + 1)])


def cut_kernel(place, gate, down, *outs):
    m, k = place[0], place[1]
    width = gate.shape[2] // 8
    for which, weight in enumerate((gate, down)):
        mine, for_k, for_m = outs[3 * which : 3 * which + 3]
        for dm, dk, out in ((0, 0, mine), (0, 1, for_k), (1, 0, for_m.at[0]), (1, 1, for_m.at[1])):
            for p in range(2):
                at = (4 * p + 2 * (m ^ dm) + (k ^ dk)) * width
                out[:, p * width : (p + 1) * width] = weight[0, :, pl.ds(pl.multiple_of(at, width), width)]


def cut_weights(gate, down):
    _, hidden, feats = gate.shape
    place = jnp.stack([lax.axis_index("m"), lax.axis_index("k")]).astype(jnp.int32)
    rows = hidden // 2
    whole = pl.BlockSpec((1, rows, feats), lambda i: (0, i, 0))
    one = pl.BlockSpec((rows, feats // 4), lambda i: (i, 0))
    two = pl.BlockSpec((2, rows, feats // 4), lambda i: (0, i, 0))
    shape = lambda *lead: jax.ShapeDtypeStruct((*lead, hidden, feats // 4), BF)
    parts = pl.pallas_call(
        cut_kernel,
        out_shape=[shape(), shape(), shape(2)] * 2,
        grid=(2,),
        in_specs=[pl.BlockSpec(memory_space=pltpu.SMEM), whole, whole],
        out_specs=[one, one, two] * 2,
        compiler_params=pltpu.CompilerParams(vmem_limit_bytes=32 << 20),
        cost_estimate=pl.CostEstimate(flops=0, bytes_accessed=4 * gate.size * 2, transcendentals=0),
    )(place, gate, down)
    return parts[:3], parts[3:]


def order(near, far):
    m = lax.axis_index("m")
    first = jnp.where(m == 0, near, far)
    second = jnp.where(m == 0, far, near)
    return jnp.concatenate([first, second], axis=0)


def slots(codes, weights, plan):
    groups, rows = codes.shape
    hosts = plan.shape[0]
    count = hosts // lax.axis_size("zh")
    experts = lax.axis_index("zh") * count + jnp.arange(count, dtype=jnp.int32)
    ids = jnp.arange(hosts, dtype=jnp.int32)
    spare_host = jnp.sum(jnp.where(plan[None, :] == experts[:, None], ids[None, :], 0), axis=1)
    here = jnp.sum(jnp.where(ids[None, :] == experts[:, None], plan[None, :], 0), axis=1)
    own_code = 2 * jnp.concatenate([experts, spare_host])
    spare_code = 2 * jnp.concatenate([here, experts]) + 1
    is_own = codes[:, None, :] == own_code[None, :, None]
    is_spare = codes[:, None, :] == spare_code[None, :, None]
    landed = is_own | is_spare
    at = jnp.arange(rows, dtype=jnp.int32)
    before = (at[:, None] < at[None, :]).astype(BF)
    position = dot(landed.astype(BF), before, ((2,), (0,)))
    fits = position < CAP
    kept = (is_own[:, :count] & fits[:, :count]) | (is_spare[:, count:] & fits[:, count:])
    rank = dot(kept.astype(BF), before, ((2,), (0,)))
    slot = jnp.arange(2 * CAP, dtype=F32)
    hit = kept[:, :, None, :] & (rank[:, :, None, :] == slot[None, None, :, None])
    token = at // TOPK + 1
    tokens_of = jnp.sum(jnp.where(hit, token[None, None, None, :], 0), axis=3)
    group = jnp.arange(groups, dtype=jnp.int32)[:, None, None]
    tokens_of = jnp.where(tokens_of > 0, tokens_of - 1 + group * (rows // TOPK), -1)
    weight_of = jnp.sum(jnp.where(hit, weights[:, None, None, :], 0.0), axis=3)
    order = lambda v: v.transpose(1, 0, 2).reshape(-1)
    return order(tokens_of), order(weight_of)


def halves(value):
    high = lax.reduce_precision(value, 8, 7)
    return high.astype(BF), (value - high).astype(BF)


def host_codes(plan):
    hosts = plan.shape[0]
    count = hosts // lax.axis_size("zh")
    experts = lax.axis_index("zh") * count + jnp.arange(count, dtype=jnp.int32)
    ids = jnp.arange(hosts, dtype=jnp.int32)
    spare_host = jnp.sum(jnp.where(plan[None, :] == experts[:, None], ids[None, :], 0), axis=1)
    here = jnp.sum(jnp.where(ids[None, :] == experts[:, None], plan[None, :], 0), axis=1)
    own_code = 2 * jnp.concatenate([experts, spare_host])
    spare_code = 2 * jnp.concatenate([here, experts]) + 1
    return jnp.stack([own_code, spare_code], axis=1).astype(F32)


def ahead(shape, axis):
    return lax.broadcasted_iota(jnp.int32, shape, axis)


def one(mask, dtype=F32):
    return jnp.where(mask, 1.0, 0.0).astype(dtype)


def route_kernel(index, group, came, codes, rows_out, high_out, mid_out):
    count, rows = codes.shape[0] // 2, group * TOPK
    feats, lines = came.shape[2], 2 * group
    before = one(ahead((rows, rows), 0) < ahead((rows, rows), 1), BF)
    own_code, spare_code = codes[:, 0:1], codes[:, 1:2]
    table = jnp.zeros((4 * count, 2 * group), F32)
    for g in range(2):
        info = came[g, lines : lines + 16, index * rows : (index + 1) * rows].astype(F32)
        code, high, mid = info[0:1], info[1:2], info[2:3]
        own, spare = one(code == own_code), one(code == spare_code)
        position = dot((own + spare).astype(BF), before, ((1,), (0,)))
        fits = position < CAP
        own, spare = jnp.where(fits, own, 0.0), jnp.where(fits, spare, 0.0)
        kept = own[:count] + spare[count:]
        rank = dot(kept.astype(BF), before, ((1,), (0,)))
        facts = jnp.concatenate([kept, kept * rank, kept * high, kept * mid], axis=0).astype(BF)
        shape = (rows, 2 * group)
        to_token = one(ahead(shape, 0) // TOPK + g * group == ahead(shape, 1), BF)
        table = table + dot(facts, to_token, ((1,), (0,)))
    table = table.astype(BF)
    slots = count * 4 * CAP
    shape = (slots, count)
    spread = one(ahead(shape, 0) // (4 * CAP) == ahead(shape, 1), BF)
    kept, rank, high, mid = (
        dot(spread, table[i * count : (i + 1) * count], ((1,), (0,))) for i in range(4)
    )
    shape = (slots, 2 * group)
    slot, token = ahead(shape, 0), ahead(shape, 1)
    turn = (slot % (2 * CAP)).astype(F32)
    hot = (kept > 0.5) & (rank == turn) & ((slot // (2 * CAP)) % 2 == token // group)
    high_out[...] = jnp.where(hot, high, 0.0).astype(BF)
    mid_out[...] = jnp.where(hot, mid, 0.0).astype(BF)
    hot = one(hot, BF)
    for p in range(2):
        both = jnp.concatenate([came[2 * p + g, index * group : (index + 1) * group] for g in range(2)], axis=0)
        rows_out[:, p * feats : (p + 1) * feats] = dot(hot, both, ((1,), (0,))).astype(BF)


def route(came, codes, index, group):
    slots, feats = codes.shape[0] // 2 * 4 * CAP, came.shape[2]
    vmem = pl.BlockSpec(memory_space=pltpu.VMEM)
    shape = lambda width: jax.ShapeDtypeStruct((slots, width), BF)
    return pl.pallas_call(
        functools.partial(route_kernel, index, group),
        out_shape=[shape(2 * feats), shape(2 * group), shape(2 * group)],
        in_specs=[vmem, vmem],
        out_specs=[vmem, vmem, vmem],
        compiler_params=pltpu.CompilerParams(vmem_limit_bytes=32 << 20),
        cost_estimate=pl.CostEstimate(flops=2 * slots * 2 * group * 2 * feats, bytes_accessed=2 << 20, transcendentals=0),
    )(came, codes)


def pack_kernel(tokens, info, out):
    count = tokens.shape[0]
    for i in range(out.shape[0]):
        out[i, :count] = tokens[...]
        out[i, count:] = info[...]


def pack(tokens, info):
    vmem = pl.BlockSpec(memory_space=pltpu.VMEM)
    return pl.pallas_call(
        pack_kernel,
        out_shape=jax.ShapeDtypeStruct((4, tokens.shape[0] + info.shape[0], tokens.shape[1]), BF),
        in_specs=[vmem, vmem],
        out_specs=vmem,
    )(tokens, info)


def gate_kernel(rows, own, other, send_out, part_out):
    send_out[...] = dot(rows[...], other[...], ((1,), (1,))).astype(BF)
    part_out[...] = dot(rows[...], own[...], ((1,), (1,)))


def down_kernel(hidden, hidden_other, own, other, out):
    total = dot(hidden[...], own[...], ((1,), (0,))) + dot(hidden_other[...], other[...], ((1,), (0,)))
    out[...] = total.astype(BF)


def on_rows(kernel, arrays, weights, widths, types):
    count = arrays[0].shape[0]
    block = count // 2
    by_rows = lambda width: pl.BlockSpec((block, width), lambda i: (i, 0))
    whole = pl.BlockSpec(memory_space=pltpu.VMEM)
    moved = sum(a.size for a in (*arrays, *weights)) * 2 + 4 * count * sum(widths)
    return pl.pallas_call(
        kernel,
        out_shape=[jax.ShapeDtypeStruct((count, width), held) for width, held in zip(widths, types)],
        grid=(2,),
        in_specs=[*(by_rows(a.shape[1]) for a in arrays), *(whole for _ in weights)],
        out_specs=[by_rows(width) for width in widths],
        compiler_params=pltpu.CompilerParams(vmem_limit_bytes=32 << 20),
        cost_estimate=pl.CostEstimate(
            flops=2 * count * sum(w.size for w in weights), bytes_accessed=moved, transcendentals=0
        ),
    )(*arrays, *weights)


def local(tokens, w_gate, w_down, expert_ids, route_weight, replica_pick, old_plan, new_plan):
    batches, group, feats = tokens.shape
    peers = lax.axis_size("y") * lax.axis_size("x")
    code = (2 * expert_ids + (replica_pick & 1)).astype(BF)
    info = jnp.stack([code, *halves(route_weight)]).reshape(3, feats)
    sent = pack(tokens.reshape(-1, feats), jnp.pad(info, ((0, 13), (0, 0))))
    came = lax.all_to_all(sent, ("p", "zh"), 0, 0, tiled=True)
    plans = [host_codes(old_plan), host_codes(new_plan)]

    gate_parts, down_parts = cut_weights(w_gate, w_down)
    came, gate_sent = lax.optimization_barrier((came, gate_parts[2]))
    gate_far = swap(gate_sent, "m")
    routed = [route(came, plans[index], index, group) for index in range(batches)]
    gate_far, routed[1] = lax.optimization_barrier((gate_far, routed[1]))
    gate_own = order(gate_parts[0], gate_far[0])
    gate_other = swap(order(gate_parts[1], gate_far[1]), "k")
    _, down_sent = lax.optimization_barrier((gate_far, down_parts[2]))
    down_far = swap(down_sent, "m")
    down_own = order(down_parts[0], down_far[0])
    down_other = swap(order(down_parts[1], down_far[1]), "k")

    outs, scales = [], []
    for index in range(batches):
        rows, high, mid = routed[index]
        scales.append((high, mid))
        rows = rows.reshape(peers, -1, rows.shape[1])
        rows = lax.all_to_all(rows, ("y", "x"), 0, 0, tiled=True).reshape(-1, rows.shape[2])
        if outs:
            rows, _ = lax.optimization_barrier((rows, outs[0]))

        cut = gate_own.shape[0]
        send, part = on_rows(gate_kernel, [rows], [gate_own, gate_other], [cut, cut], [BF, F32])
        part = part + swap(send, "k").astype(F32)
        gate = part + swap(part.astype(BF), "m").astype(F32)
        hidden = jax.nn.silu(gate).astype(BF)
        hidden_other = swap(hidden, "k")
        (out,) = on_rows(down_kernel, [hidden, hidden_other], [down_own, down_other], [rows.shape[1]], [BF])
        outs.append(out.reshape(peers, -1, out.shape[1]))

    outputs = []
    for out, (high, mid) in zip(outs, scales):
        back = lax.all_to_all(out, ("y", "x"), 0, 0, tiled=True).reshape(-1, out.shape[2])
        mixed = dot(high, back, ((0,), (0,))) + dot(mid, back, ((0,), (0,)))
        outputs.append(mixed.astype(BF).reshape(2, group, 2, feats))
    mixed = jnp.stack(outputs).transpose(3, 1, 0, 2, 4).reshape(4, batches * group, feats)
    terms = lax.all_to_all(mixed, ("p", "zh"), 0, 0, tiled=True)
    return jnp.sum(terms.astype(F32), axis=0).astype(BF).reshape(batches, group, feats)


def solution(mesh):
    names = tuple(name for name, _ in SPLIT)
    cut = Mesh(mesh.devices.reshape([size for _, size in SPLIT]), names)
    dp, expert = ("p", "m", "k"), ("zh", "y", "x")
    placed = (
        P(None, expert, dp),
        P(expert, dp, None),
        P(expert, dp, None),
        P(None, expert, None),
        P(None, expert, None),
        P(None, expert, None),
        P(),
        P(),
    )
    return jax.shard_map(
        local, mesh=cut, in_specs=placed, out_specs=P(None, expert, dp), check_vma=False
    )
```

```python
import functools

import jax
import jax.numpy as jnp
from jax import lax
from jax.experimental import pallas as pl
from jax.experimental.pallas import tpu as pltpu
from jax.sharding import Mesh
from jax.sharding import PartitionSpec as P

TOPK = 8
CAP = 4
BF = jnp.bfloat16
F32 = jnp.float32

SPLIT = (("p", 2), ("m", 2), ("k", 2), ("zh", 2), ("y", 8), ("x", 4))


def dot(a, b, dims, out=F32):
    return lax.dot_general(a, b, (dims, ((), ())), preferred_element_type=out)


def swap(array, *axes):
    last = 2 ** len(axes) - 1
    return lax.ppermute(array, axes, [(i, last - i) for i in range(last + 1)])


def cut_kernel(place, gate, down, *outs):
    m, k = place[0], place[1]
    width = gate.shape[2] // 8
    for which, weight in enumerate((gate, down)):
        mine, for_k, for_m = outs[3 * which : 3 * which + 3]
        for dm, dk, out in ((0, 0, mine), (0, 1, for_k), (1, 0, for_m.at[0]), (1, 1, for_m.at[1])):
            for p in range(2):
                at = (4 * p + 2 * (m ^ dm) + (k ^ dk)) * width
                out[:, p * width : (p + 1) * width] = weight[0, :, pl.ds(pl.multiple_of(at, width), width)]


def cut_weights(gate, down):
    _, hidden, feats = gate.shape
    place = jnp.stack([lax.axis_index("m"), lax.axis_index("k")]).astype(jnp.int32)
    rows = hidden // 2
    whole = pl.BlockSpec((1, rows, feats), lambda i: (0, i, 0))
    one = pl.BlockSpec((rows, feats // 4), lambda i: (i, 0))
    two = pl.BlockSpec((2, rows, feats // 4), lambda i: (0, i, 0))
    shape = lambda *lead: jax.ShapeDtypeStruct((*lead, hidden, feats // 4), BF)
    parts = pl.pallas_call(
        cut_kernel,
        out_shape=[shape(), shape(), shape(2)] * 2,
        grid=(2,),
        in_specs=[pl.BlockSpec(memory_space=pltpu.SMEM), whole, whole],
        out_specs=[one, one, two] * 2,
        compiler_params=pltpu.CompilerParams(vmem_limit_bytes=32 << 20),
        cost_estimate=pl.CostEstimate(flops=0, bytes_accessed=4 * gate.size * 2, transcendentals=0),
    )(place, gate, down)
    return parts[:3], parts[3:]


def order(near, far):
    m = lax.axis_index("m")
    first = jnp.where(m == 0, near, far)
    second = jnp.where(m == 0, far, near)
    return jnp.concatenate([first, second], axis=0)


def slots(codes, weights, plan):
    groups, rows = codes.shape
    hosts = plan.shape[0]
    count = hosts // lax.axis_size("zh")
    experts = lax.axis_index("zh") * count + jnp.arange(count, dtype=jnp.int32)
    ids = jnp.arange(hosts, dtype=jnp.int32)
    spare_host = jnp.sum(jnp.where(plan[None, :] == experts[:, None], ids[None, :], 0), axis=1)
    here = jnp.sum(jnp.where(ids[None, :] == experts[:, None], plan[None, :], 0), axis=1)
    own_code = 2 * jnp.concatenate([experts, spare_host])
    spare_code = 2 * jnp.concatenate([here, experts]) + 1
    is_own = codes[:, None, :] == own_code[None, :, None]
    is_spare = codes[:, None, :] == spare_code[None, :, None]
    landed = is_own | is_spare
    at = jnp.arange(rows, dtype=jnp.int32)
    before = (at[:, None] < at[None, :]).astype(BF)
    position = dot(landed.astype(BF), before, ((2,), (0,)))
    fits = position < CAP
    kept = (is_own[:, :count] & fits[:, :count]) | (is_spare[:, count:] & fits[:, count:])
    rank = dot(kept.astype(BF), before, ((2,), (0,)))
    slot = jnp.arange(2 * CAP, dtype=F32)
    hit = kept[:, :, None, :] & (rank[:, :, None, :] == slot[None, None, :, None])
    token = at // TOPK + 1
    tokens_of = jnp.sum(jnp.where(hit, token[None, None, None, :], 0), axis=3)
    group = jnp.arange(groups, dtype=jnp.int32)[:, None, None]
    tokens_of = jnp.where(tokens_of > 0, tokens_of - 1 + group * (rows // TOPK), -1)
    weight_of = jnp.sum(jnp.where(hit, weights[:, None, None, :], 0.0), axis=3)
    order = lambda v: v.transpose(1, 0, 2).reshape(-1)
    return order(tokens_of), order(weight_of)


def halves(value):
    high = lax.reduce_precision(value, 8, 7)
    return high.astype(BF), (value - high).astype(BF)


def host_codes(plan):
    hosts = plan.shape[0]
    count = hosts // lax.axis_size("zh")
    experts = lax.axis_index("zh") * count + jnp.arange(count, dtype=jnp.int32)
    ids = jnp.arange(hosts, dtype=jnp.int32)
    spare_host = jnp.sum(jnp.where(plan[None, :] == experts[:, None], ids[None, :], 0), axis=1)
    here = jnp.sum(jnp.where(ids[None, :] == experts[:, None], plan[None, :], 0), axis=1)
    own_code = 2 * jnp.concatenate([experts, spare_host])
    spare_code = 2 * jnp.concatenate([here, experts]) + 1
    return jnp.stack([own_code, spare_code], axis=1).astype(F32)


def ahead(shape, axis):
    return lax.broadcasted_iota(jnp.int32, shape, axis)


def one(mask, dtype=F32):
    return jnp.where(mask, 1.0, 0.0).astype(dtype)


def route_kernel(index, group, came, codes, rows_out, high_out, mid_out):
    count, rows = codes.shape[0] // 2, group * TOPK
    feats, lines = came.shape[2], 2 * group
    before = one(ahead((rows, rows), 0) < ahead((rows, rows), 1), BF)
    own_code, spare_code = codes[:, 0:1], codes[:, 1:2]
    table = jnp.zeros((4 * count, 2 * group), F32)
    for g in range(2):
        info = came[g, lines : lines + 16, index * rows : (index + 1) * rows].astype(F32)
        code, high, mid = info[0:1], info[1:2], info[2:3]
        own, spare = one(code == own_code), one(code == spare_code)
        position = dot((own + spare).astype(BF), before, ((1,), (0,)))
        fits = position < CAP
        own, spare = jnp.where(fits, own, 0.0), jnp.where(fits, spare, 0.0)
        kept = own[:count] + spare[count:]
        rank = dot(kept.astype(BF), before, ((1,), (0,)))
        facts = jnp.concatenate([kept, kept * rank, kept * high, kept * mid], axis=0).astype(BF)
        shape = (rows, 2 * group)
        to_token = one(ahead(shape, 0) // TOPK + g * group == ahead(shape, 1), BF)
        table = table + dot(facts, to_token, ((1,), (0,)))
    table = table.astype(BF)
    slots = count * 4 * CAP
    shape = (slots, count)
    spread = one(ahead(shape, 0) // (4 * CAP) == ahead(shape, 1), BF)
    kept, rank, high, mid = (
        dot(spread, table[i * count : (i + 1) * count], ((1,), (0,))) for i in range(4)
    )
    shape = (slots, 2 * group)
    slot, token = ahead(shape, 0), ahead(shape, 1)
    turn = (slot % (2 * CAP)).astype(F32)
    hot = (kept > 0.5) & (rank == turn) & ((slot // (2 * CAP)) % 2 == token // group)
    high_out[...] = jnp.where(hot, high, 0.0).astype(BF)
    mid_out[...] = jnp.where(hot, mid, 0.0).astype(BF)
    hot = one(hot, BF)
    for p in range(2):
        both = jnp.concatenate([came[2 * p + g, index * group : (index + 1) * group] for g in range(2)], axis=0)
        rows_out[:, p * feats : (p + 1) * feats] = dot(hot, both, ((1,), (0,))).astype(BF)


def route(came, codes, index, group):
    slots, feats = codes.shape[0] // 2 * 4 * CAP, came.shape[2]
    vmem = pl.BlockSpec(memory_space=pltpu.VMEM)
    shape = lambda width: jax.ShapeDtypeStruct((slots, width), BF)
    return pl.pallas_call(
        functools.partial(route_kernel, index, group),
        out_shape=[shape(2 * feats), shape(2 * group), shape(2 * group)],
        in_specs=[vmem, vmem],
        out_specs=[vmem, vmem, vmem],
        compiler_params=pltpu.CompilerParams(vmem_limit_bytes=32 << 20),
        cost_estimate=pl.CostEstimate(flops=2 * slots * 2 * group * 2 * feats, bytes_accessed=2 << 20, transcendentals=0),
    )(came, codes)


def order_kernel(place, near, far, out):
    m, hidden = place[0], near.shape[0]
    out[pl.ds(pl.multiple_of(m * hidden, 64), hidden)] = near[...]
    out[pl.ds(pl.multiple_of((1 - m) * hidden, 64), hidden)] = far[0]


def ordered(near, far, which):
    hidden, wide = near.shape
    place = lax.axis_index("m").astype(jnp.int32).reshape(1)
    return pl.pallas_call(
        order_kernel,
        out_shape=jax.ShapeDtypeStruct((2 * hidden, wide), BF),
        grid=(1,),
        in_specs=[
            pl.BlockSpec(memory_space=pltpu.SMEM),
            pl.BlockSpec((hidden, wide), lambda i: (0, 0)),
            pl.BlockSpec((1, hidden, wide), lambda i: (which, 0, 0)),
        ],
        out_specs=pl.BlockSpec((2 * hidden, wide), lambda i: (0, 0)),
        compiler_params=pltpu.CompilerParams(vmem_limit_bytes=32 << 20),
        cost_estimate=pl.CostEstimate(flops=0, bytes_accessed=8 * near.size, transcendentals=0),
    )(place, near, far)


def gate_kernel(rows, own, other, send_out, part_out):
    send_out[...] = dot(rows[...], other[...], ((1,), (1,))).astype(BF)
    part_out[...] = dot(rows[...], own[...], ((1,), (1,)))


def down_kernel(hidden, hidden_other, own, other, out):
    total = dot(hidden[...], own[...], ((1,), (0,))) + dot(hidden_other[...], other[...], ((1,), (0,)))
    out[...] = total.astype(BF)


def on_rows(kernel, arrays, weights, widths, types):
    count = arrays[0].shape[0]
    block = count // 2
    by_rows = lambda width: pl.BlockSpec((block, width), lambda i: (i, 0))
    whole = pl.BlockSpec(memory_space=pltpu.VMEM)
    moved = sum(a.size for a in (*arrays, *weights)) * 2 + 4 * count * sum(widths)
    return pl.pallas_call(
        kernel,
        out_shape=[jax.ShapeDtypeStruct((count, width), held) for width, held in zip(widths, types)],
        grid=(2,),
        in_specs=[*(by_rows(a.shape[1]) for a in arrays), *(whole for _ in weights)],
        out_specs=[by_rows(width) for width in widths],
        compiler_params=pltpu.CompilerParams(vmem_limit_bytes=32 << 20),
        cost_estimate=pl.CostEstimate(
            flops=2 * count * sum(w.size for w in weights), bytes_accessed=moved, transcendentals=0
        ),
    )(*arrays, *weights)


def local(tokens, w_gate, w_down, expert_ids, route_weight, replica_pick, old_plan, new_plan):
    batches, group, feats = tokens.shape
    peers = lax.axis_size("y") * lax.axis_size("x")
    code = (2 * expert_ids + (replica_pick & 1)).astype(BF)
    info = jnp.stack([code, *halves(route_weight)]).reshape(3, feats)
    sent = jnp.concatenate([tokens.reshape(-1, feats), jnp.pad(info, ((0, 13), (0, 0)))])
    sent = jnp.broadcast_to(sent[None], (4, *sent.shape))
    came = lax.all_to_all(sent, ("p", "zh"), 0, 0, tiled=True)
    plans = [host_codes(old_plan), host_codes(new_plan)]

    gate_parts, down_parts = cut_weights(w_gate, w_down)
    came, gate_sent = lax.optimization_barrier((came, gate_parts[2]))
    gate_far = swap(gate_sent, "m")
    routed = [route(came, plans[index], index, group) for index in range(batches)]
    gate_far, routed[1] = lax.optimization_barrier((gate_far, routed[1]))
    gate_own = order(gate_parts[0], gate_far[0])
    gate_other = swap(ordered(gate_parts[1], gate_far, 1), "k")
    _, down_sent = lax.optimization_barrier((gate_far, down_parts[2]))
    down_far = swap(down_sent, "m")
    down_own = order(down_parts[0], down_far[0])
    down_other = swap(order(down_parts[1], down_far[1]), "k")

    outs, scales = [], []
    for index in range(batches):
        rows, high, mid = routed[index]
        scales.append((high, mid))
        rows = rows.reshape(peers, -1, rows.shape[1])
        rows = lax.all_to_all(rows, ("y", "x"), 0, 0, tiled=True).reshape(-1, rows.shape[2])
        if outs:
            rows, _ = lax.optimization_barrier((rows, outs[0]))

        cut = gate_own.shape[0]
        send, part = on_rows(gate_kernel, [rows], [gate_own, gate_other], [cut, cut], [BF, F32])
        part = part + swap(send, "k").astype(F32)
        gate = part + swap(part.astype(BF), "m").astype(F32)
        hidden = jax.nn.silu(gate).astype(BF)
        hidden_other = swap(hidden, "k")
        (out,) = on_rows(down_kernel, [hidden, hidden_other], [down_own, down_other], [rows.shape[1]], [BF])
        outs.append(out.reshape(peers, -1, out.shape[1]))

    outputs = []
    for out, (high, mid) in zip(outs, scales):
        back = lax.all_to_all(out, ("y", "x"), 0, 0, tiled=True).reshape(-1, out.shape[2])
        mixed = dot(high, back, ((0,), (0,))) + dot(mid, back, ((0,), (0,)))
        outputs.append(mixed.astype(BF).reshape(2, group, 2, feats))
    mixed = jnp.stack(outputs).transpose(3, 1, 0, 2, 4).reshape(4, batches * group, feats)
    terms = lax.all_to_all(mixed, ("p", "zh"), 0, 0, tiled=True)
    return jnp.sum(terms.astype(F32), axis=0).astype(BF).reshape(batches, group, feats)


def solution(mesh):
    names = tuple(name for name, _ in SPLIT)
    cut = Mesh(mesh.devices.reshape([size for _, size in SPLIT]), names)
    dp, expert = ("p", "m", "k"), ("zh", "y", "x")
    placed = (
        P(None, expert, dp),
        P(expert, dp, None),
        P(expert, dp, None),
        P(None, expert, None),
        P(None, expert, None),
        P(None, expert, None),
        P(),
        P(),
    )
    return jax.shard_map(
        local, mesh=cut, in_specs=placed, out_specs=P(None, expert, dp), check_vma=False
    )
```

```python
import functools

import jax
import jax.numpy as jnp
from jax import lax
from jax.experimental import pallas as pl
from jax.experimental.pallas import tpu as pltpu
from jax.sharding import Mesh
from jax.sharding import PartitionSpec as P

TOPK = 8
CAP = 4
BF = jnp.bfloat16
F32 = jnp.float32

SPLIT = (("p", 2), ("m", 2), ("k", 2), ("zh", 2), ("y", 8), ("x", 4))


def dot(a, b, dims, out=F32):
    return lax.dot_general(a, b, (dims, ((), ())), preferred_element_type=out)


def swap(array, *axes):
    last = 2 ** len(axes) - 1
    return lax.ppermute(array, axes, [(i, last - i) for i in range(last + 1)])


def cut_kernel(place, gate, down, *outs):
    m, k = place[0], place[1]
    width = gate.shape[2] // 8
    for which, weight in enumerate((gate, down)):
        mine, for_k, for_m = outs[3 * which : 3 * which + 3]
        for dm, dk, out in ((0, 0, mine), (0, 1, for_k), (1, 0, for_m.at[0]), (1, 1, for_m.at[1])):
            for p in range(2):
                at = (4 * p + 2 * (m ^ dm) + (k ^ dk)) * width
                out[:, p * width : (p + 1) * width] = weight[0, :, pl.ds(pl.multiple_of(at, width), width)]


def cut_weights(gate, down):
    _, hidden, feats = gate.shape
    place = jnp.stack([lax.axis_index("m"), lax.axis_index("k")]).astype(jnp.int32)
    rows = hidden // 2
    whole = pl.BlockSpec((1, rows, feats), lambda i: (0, i, 0))
    one = pl.BlockSpec((rows, feats // 4), lambda i: (i, 0))
    two = pl.BlockSpec((2, rows, feats // 4), lambda i: (0, i, 0))
    shape = lambda *lead: jax.ShapeDtypeStruct((*lead, hidden, feats // 4), BF)
    parts = pl.pallas_call(
        cut_kernel,
        out_shape=[shape(), shape(), shape(2)] * 2,
        grid=(2,),
        in_specs=[pl.BlockSpec(memory_space=pltpu.SMEM), whole, whole],
        out_specs=[one, one, two] * 2,
        compiler_params=pltpu.CompilerParams(vmem_limit_bytes=32 << 20),
        cost_estimate=pl.CostEstimate(flops=0, bytes_accessed=4 * gate.size * 2, transcendentals=0),
    )(place, gate, down)
    return parts[:3], parts[3:]


def order(near, far):
    m = lax.axis_index("m")
    first = jnp.where(m == 0, near, far)
    second = jnp.where(m == 0, far, near)
    return jnp.concatenate([first, second], axis=0)


def slots(codes, weights, plan):
    groups, rows = codes.shape
    hosts = plan.shape[0]
    count = hosts // lax.axis_size("zh")
    experts = lax.axis_index("zh") * count + jnp.arange(count, dtype=jnp.int32)
    ids = jnp.arange(hosts, dtype=jnp.int32)
    spare_host = jnp.sum(jnp.where(plan[None, :] == experts[:, None], ids[None, :], 0), axis=1)
    here = jnp.sum(jnp.where(ids[None, :] == experts[:, None], plan[None, :], 0), axis=1)
    own_code = 2 * jnp.concatenate([experts, spare_host])
    spare_code = 2 * jnp.concatenate([here, experts]) + 1
    is_own = codes[:, None, :] == own_code[None, :, None]
    is_spare = codes[:, None, :] == spare_code[None, :, None]
    landed = is_own | is_spare
    at = jnp.arange(rows, dtype=jnp.int32)
    before = (at[:, None] < at[None, :]).astype(BF)
    position = dot(landed.astype(BF), before, ((2,), (0,)))
    fits = position < CAP
    kept = (is_own[:, :count] & fits[:, :count]) | (is_spare[:, count:] & fits[:, count:])
    rank = dot(kept.astype(BF), before, ((2,), (0,)))
    slot = jnp.arange(2 * CAP, dtype=F32)
    hit = kept[:, :, None, :] & (rank[:, :, None, :] == slot[None, None, :, None])
    token = at // TOPK + 1
    tokens_of = jnp.sum(jnp.where(hit, token[None, None, None, :], 0), axis=3)
    group = jnp.arange(groups, dtype=jnp.int32)[:, None, None]
    tokens_of = jnp.where(tokens_of > 0, tokens_of - 1 + group * (rows // TOPK), -1)
    weight_of = jnp.sum(jnp.where(hit, weights[:, None, None, :], 0.0), axis=3)
    order = lambda v: v.transpose(1, 0, 2).reshape(-1)
    return order(tokens_of), order(weight_of)


def halves(value):
    high = lax.reduce_precision(value, 8, 7)
    return high.astype(BF), (value - high).astype(BF)


def host_codes(plan):
    hosts = plan.shape[0]
    count = hosts // lax.axis_size("zh")
    experts = lax.axis_index("zh") * count + jnp.arange(count, dtype=jnp.int32)
    ids = jnp.arange(hosts, dtype=jnp.int32)
    spare_host = jnp.sum(jnp.where(plan[None, :] == experts[:, None], ids[None, :], 0), axis=1)
    here = jnp.sum(jnp.where(ids[None, :] == experts[:, None], plan[None, :], 0), axis=1)
    own_code = 2 * jnp.concatenate([experts, spare_host])
    spare_code = 2 * jnp.concatenate([here, experts]) + 1
    return jnp.stack([own_code, spare_code], axis=1).astype(F32)


def ahead(shape, axis):
    return lax.broadcasted_iota(jnp.int32, shape, axis)


def one(mask, dtype=F32):
    return jnp.where(mask, 1.0, 0.0).astype(dtype)


def route_kernel(index, group, came, codes, rows_out, high_out, mid_out):
    count, rows = codes.shape[0] // 2, group * TOPK
    feats, lines = came.shape[2], 2 * group
    before = one(ahead((rows, rows), 0) < ahead((rows, rows), 1), BF)
    own_code, spare_code = codes[:, 0:1], codes[:, 1:2]
    table = jnp.zeros((4 * count, 2 * group), F32)
    for g in range(2):
        info = came[g, lines : lines + 16, index * rows : (index + 1) * rows].astype(F32)
        code, high, mid = info[0:1], info[1:2], info[2:3]
        own, spare = one(code == own_code), one(code == spare_code)
        position = dot((own + spare).astype(BF), before, ((1,), (0,)))
        fits = position < CAP
        own, spare = jnp.where(fits, own, 0.0), jnp.where(fits, spare, 0.0)
        kept = own[:count] + spare[count:]
        rank = dot(kept.astype(BF), before, ((1,), (0,)))
        facts = jnp.concatenate([kept, kept * rank, kept * high, kept * mid], axis=0).astype(BF)
        shape = (rows, 2 * group)
        to_token = one(ahead(shape, 0) // TOPK + g * group == ahead(shape, 1), BF)
        table = table + dot(facts, to_token, ((1,), (0,)))
    table = table.astype(BF)
    slots = count * 4 * CAP
    shape = (slots, count)
    spread = one(ahead(shape, 0) // (4 * CAP) == ahead(shape, 1), BF)
    kept, rank, high, mid = (
        dot(spread, table[i * count : (i + 1) * count], ((1,), (0,))) for i in range(4)
    )
    shape = (slots, 2 * group)
    slot, token = ahead(shape, 0), ahead(shape, 1)
    turn = (slot % (2 * CAP)).astype(F32)
    hot = (kept > 0.5) & (rank == turn) & ((slot // (2 * CAP)) % 2 == token // group)
    high_out[...] = jnp.where(hot, high, 0.0).astype(BF)
    mid_out[...] = jnp.where(hot, mid, 0.0).astype(BF)
    hot = one(hot, BF)
    for p in range(2):
        both = jnp.concatenate([came[2 * p + g, index * group : (index + 1) * group] for g in range(2)], axis=0)
        rows_out[:, p * feats : (p + 1) * feats] = dot(hot, both, ((1,), (0,))).astype(BF)


def route(came, codes, index, group):
    slots, feats = codes.shape[0] // 2 * 4 * CAP, came.shape[2]
    vmem = pl.BlockSpec(memory_space=pltpu.VMEM)
    shape = lambda width: jax.ShapeDtypeStruct((slots, width), BF)
    return pl.pallas_call(
        functools.partial(route_kernel, index, group),
        out_shape=[shape(2 * feats), shape(2 * group), shape(2 * group)],
        in_specs=[vmem, vmem],
        out_specs=[vmem, vmem, vmem],
        compiler_params=pltpu.CompilerParams(vmem_limit_bytes=32 << 20),
        cost_estimate=pl.CostEstimate(flops=2 * slots * 2 * group * 2 * feats, bytes_accessed=2 << 20, transcendentals=0),
    )(came, codes)


def order_kernel(place, near, far, out):
    m, hidden = place[0], near.shape[0]
    out[pl.ds(pl.multiple_of(m * hidden, 64), hidden)] = near[...]
    out[pl.ds(pl.multiple_of((1 - m) * hidden, 64), hidden)] = far[0]


def ordered(near, far, which):
    hidden, wide = near.shape
    place = lax.axis_index("m").astype(jnp.int32).reshape(1)
    return pl.pallas_call(
        order_kernel,
        out_shape=jax.ShapeDtypeStruct((2 * hidden, wide), BF),
        grid=(1,),
        in_specs=[
            pl.BlockSpec(memory_space=pltpu.SMEM),
            pl.BlockSpec((hidden, wide), lambda i: (0, 0)),
            pl.BlockSpec((1, hidden, wide), lambda i: (which, 0, 0)),
        ],
        out_specs=pl.BlockSpec((2 * hidden, wide), lambda i: (0, 0)),
        compiler_params=pltpu.CompilerParams(vmem_limit_bytes=32 << 20),
        cost_estimate=pl.CostEstimate(flops=0, bytes_accessed=8 * near.size, transcendentals=0),
    )(place, near, far)


def gate_kernel(rows, own, other, send_out, part_out):
    send_out[...] = dot(rows[...], other[...], ((1,), (1,))).astype(BF)
    part_out[...] = dot(rows[...], own[...], ((1,), (1,)))


def down_kernel(hidden, hidden_other, own, other, out):
    total = dot(hidden[...], own[...], ((1,), (0,))) + dot(hidden_other[...], other[...], ((1,), (0,)))
    out[...] = total.astype(BF)


def on_rows(kernel, arrays, weights, widths, types):
    count = arrays[0].shape[0]
    block = count // 2
    by_rows = lambda width: pl.BlockSpec((block, width), lambda i: (i, 0))
    whole = pl.BlockSpec(memory_space=pltpu.VMEM)
    moved = sum(a.size for a in (*arrays, *weights)) * 2 + 4 * count * sum(widths)
    return pl.pallas_call(
        kernel,
        out_shape=[jax.ShapeDtypeStruct((count, width), held) for width, held in zip(widths, types)],
        grid=(2,),
        in_specs=[*(by_rows(a.shape[1]) for a in arrays), *(whole for _ in weights)],
        out_specs=[by_rows(width) for width in widths],
        compiler_params=pltpu.CompilerParams(vmem_limit_bytes=32 << 20),
        cost_estimate=pl.CostEstimate(
            flops=2 * count * sum(w.size for w in weights), bytes_accessed=moved, transcendentals=0
        ),
    )(*arrays, *weights)


def local(tokens, w_gate, w_down, expert_ids, route_weight, replica_pick, old_plan, new_plan):
    batches, group, feats = tokens.shape
    peers = lax.axis_size("y") * lax.axis_size("x")
    code = (2 * expert_ids + (replica_pick & 1)).astype(BF)
    info = jnp.stack([code, *halves(route_weight)]).reshape(3, feats)
    sent = jnp.concatenate([tokens.reshape(-1, feats), jnp.pad(info, ((0, 13), (0, 0)))])
    sent = jnp.broadcast_to(sent[None], (4, *sent.shape))
    came = lax.all_to_all(sent, ("p", "zh"), 0, 0, tiled=True)
    plans = [host_codes(old_plan), host_codes(new_plan)]

    gate_parts, down_parts = cut_weights(w_gate, w_down)
    came, gate_sent = lax.optimization_barrier((came, gate_parts[2]))
    gate_far = swap(gate_sent, "m")
    routed = [route(came, plans[index], index, group) for index in range(batches)]
    gate_far, routed[1] = lax.optimization_barrier((gate_far, routed[1]))
    gate_other = swap(ordered(gate_parts[1], gate_far, 1), "k")
    gate_mine, gate_near, gate_other = lax.optimization_barrier((gate_parts[0], gate_far, gate_other))
    gate_own = ordered(gate_mine, gate_near, 0)
    _, down_sent = lax.optimization_barrier((gate_far, down_parts[2]))
    down_far = swap(down_sent, "m")
    down_own = order(down_parts[0], down_far[0])
    down_other = swap(order(down_parts[1], down_far[1]), "k")

    outs, scales = [], []
    for index in range(batches):
        rows, high, mid = routed[index]
        scales.append((high, mid))
        rows = rows.reshape(peers, -1, rows.shape[1])
        rows = lax.all_to_all(rows, ("y", "x"), 0, 0, tiled=True).reshape(-1, rows.shape[2])
        if outs:
            rows, _ = lax.optimization_barrier((rows, outs[0]))

        cut = gate_own.shape[0]
        send, part = on_rows(gate_kernel, [rows], [gate_own, gate_other], [cut, cut], [BF, F32])
        part = part + swap(send, "k").astype(F32)
        gate = part + swap(part.astype(BF), "m").astype(F32)
        hidden = jax.nn.silu(gate).astype(BF)
        hidden_other = swap(hidden, "k")
        (out,) = on_rows(down_kernel, [hidden, hidden_other], [down_own, down_other], [rows.shape[1]], [BF])
        outs.append(out.reshape(peers, -1, out.shape[1]))

    outputs = []
    for out, (high, mid) in zip(outs, scales):
        back = lax.all_to_all(out, ("y", "x"), 0, 0, tiled=True).reshape(-1, out.shape[2])
        mixed = dot(high, back, ((0,), (0,))) + dot(mid, back, ((0,), (0,)))
        outputs.append(mixed.astype(BF).reshape(2, group, 2, feats))
    mixed = jnp.stack(outputs).transpose(3, 1, 0, 2, 4).reshape(4, batches * group, feats)
    terms = lax.all_to_all(mixed, ("p", "zh"), 0, 0, tiled=True)
    return jnp.sum(terms.astype(F32), axis=0).astype(BF).reshape(batches, group, feats)


def solution(mesh):
    names = tuple(name for name, _ in SPLIT)
    cut = Mesh(mesh.devices.reshape([size for _, size in SPLIT]), names)
    dp, expert = ("p", "m", "k"), ("zh", "y", "x")
    placed = (
        P(None, expert, dp),
        P(expert, dp, None),
        P(expert, dp, None),
        P(None, expert, None),
        P(None, expert, None),
        P(None, expert, None),
        P(),
        P(),
    )
    return jax.shard_map(
        local, mesh=cut, in_specs=placed, out_specs=P(None, expert, dp), check_vma=False
    )
```
